512 devices in a mesh: layer: 8 (over z), row: 64 (over x, y, core).
Axes of the slice: x: 4, y: 8, z: 8, core: 2. Of those that a mesh axis runs over, the one named last changes fastest.
Arguments:
- leaf_rhs: float32 [8, 64, 256, 384], P('layer', 'row'), may hold values from -6 to 6
- leaf_inverse: float32 [8, 64, 256, 256], P('layer', 'row'), may hold values from -0.375 to 0.375
- leaf_coupling: float32 [8, 64, 4, 512, 256], P('layer', 'row'), may hold values from -0.046875 to 0.046875
- parent: int32 [8, 64], P('layer', 'row'), may hold values from 0 to 3
- sep_rhs: float32 [8, 4, 512, 384], P('layer', None, 'row'), may hold values from -6 to 6
- sep_inverse: float32 [8, 4, 512, 512], P('layer', None, 'row'), may hold values from -0.25 to 0.25
- sep_coupling: float32 [8, 3, 512, 512], P('layer', None, 'row'), may hold values from -0.125 to 0.125
- root_coupling: float32 [8, 512, 512], P('layer', 'row'), may hold values from -0.09375 to 0.09375
- root_rhs: float32 [512, 384], P('row'), may hold values from -6 to 6
- root_inverse: float32 [512, 512], P('row'), may hold values from -0.25 to 0.25
Outputs:
- sep_solution: float32 [8, 4, 512, 384], P('layer', None, 'row')
- root_solution: float32 [512, 384], P('row')
The draws below stay inside these ranges and needn't reach their ends.
All inputs are finite; a program needn't handle non-finite values.
Results may differ from the reference program's by a relative error of at most 0.0003.
Values sent between devices are 32-bit elements; how exact they have to be, the bound alone decides.
No kernel may reach another device: no remote copies, remote signals or barrier semaphores. Data moves between devices by JAX's collectives and lax.ppermute only.
A program may use at most 64 MiB of HBM per device.

```python
import jax
import jax.numpy as jnp
from jax import lax

W = 512
SEPS = 4
LEAF = 256
R = 384
N_LAYER = 8
N_ROW = 64


def with_ends(array, own_key, low, largest):
    index_at = [jax.random.randint(jax.random.fold_in(own_key, axis), (), 0, length) for axis, length in enumerate(array.shape)]
    widest = array.shape.index(max(array.shape))
    beside = index_at[:widest] + [(index_at[widest] + 1) % array.shape[widest]] + index_at[widest + 1:]
    return array.at[tuple(index_at)].set(low).at[tuple(beside)].set(largest)


def block_levels(rng, dims, shards, low, largest):
    def one(position, shards_of):
        steps = jax.random.uniform(jax.random.fold_in(jax.random.fold_in(rng, 6), position), (shards_of,), jnp.float32, low / len(shards), largest / len(shards))
        return jnp.repeat(jnp.exp(steps), dims[position] // shards_of).reshape((-1,) + (1,) * (len(dims) - position - 1))

    factor_of = one(*shards[0])
    for cut in shards[1:]:
        factor_of = factor_of * one(*cut)
    return factor_of


def normal_values(own_key, shape, scale, bound, cuts=(), kind=jnp.bfloat16):
    factor_of = block_levels(own_key, shape, cuts, -0.22, 0.18) if cuts else 1.0
    values = jax.random.normal(own_key, shape, jnp.float32) * scale * factor_of
    return jnp.minimum(jnp.maximum(values, -bound), bound).astype(kind)


def setup_inputs(seed: int = 0) -> dict:
    seeds = jax.random.split(jax.random.key(seed), 11)
    return {
        "leaf_rhs": normal_values(seeds[0], (N_LAYER, N_ROW, LEAF, R), 1.0, 6.0, ((0, 8), (1, 64)), jnp.float32),
        "leaf_inverse": normal_values(seeds[1], (N_LAYER, N_ROW, LEAF, LEAF), LEAF ** -0.5, 0.375, ((0, 8), (1, 64)), jnp.float32),
        "leaf_coupling": normal_values(seeds[2], (N_LAYER, N_ROW, SEPS, W, LEAF), (LEAF * N_ROW) ** -0.5, 0.046875, ((0, 8), (1, 64)), jnp.float32),
        "parent": with_ends(jax.random.randint(seeds[3], (N_LAYER, N_ROW), 0, SEPS), jax.random.fold_in(seeds[3], 1), 0, SEPS - 1).astype(jnp.int32),
        "sep_rhs": normal_values(seeds[4], (N_LAYER, SEPS, W, R), 1.0, 6.0, ((0, 8), (2, 64)), jnp.float32),
        "sep_inverse": normal_values(seeds[5], (N_LAYER, SEPS, W, W), W ** -0.5, 0.25, ((0, 8), (2, 64)), jnp.float32),
        "sep_coupling": normal_values(seeds[6], (N_LAYER, SEPS - 1, W, W), (4 * W) ** -0.5, 0.125, ((0, 8), (2, 64)), jnp.float32),
        "root_coupling": normal_values(seeds[7], (N_LAYER, W, W), (W * N_LAYER) ** -0.5, 0.09375, ((0, 8), (1, 64)), jnp.float32),
        "root_rhs": normal_values(seeds[8], (W, R), 1.0, 6.0, ((0, 64),), jnp.float32),
        "root_inverse": normal_values(seeds[9], (W, W), W ** -0.5, 0.25, ((0, 64),), jnp.float32),
    }


def reference(leaf_rhs, leaf_inverse, leaf_coupling, parent, sep_rhs, sep_inverse, sep_coupling, root_coupling, root_rhs, root_inverse):
    highest = lax.Precision.HIGHEST

    def one_layer(inputs):
        rhs_layer, inverse_layer, coupling_layer, parent_layer, sep_rhs_layer, sep_inverse_layer, chain_layer = inputs
        leaf_solution = jnp.einsum('rab,rbc->rac', inverse_layer, rhs_layer, precision=highest)
        levels = jnp.arange(SEPS, dtype=jnp.int32)
        keep_mask = (levels[None, :] >= parent_layer[:, None]).astype(jnp.float32)
        coupled = jnp.einsum('rkwb,rbc,rk->kwc', coupling_layer, leaf_solution, keep_mask, precision=highest)
        residual = sep_rhs_layer - coupled
        solved = []
        previous = None
        for k in range(SEPS):
            current = jnp.dot(sep_inverse_layer[k], residual[k], precision=highest)
            if k > 0:
                current = current - jnp.dot(chain_layer[k - 1], previous, precision=highest)
            solved.append(current)
            previous = current
        return jnp.stack(solved)

    sep_solution = lax.map(one_layer, (leaf_rhs, leaf_inverse, leaf_coupling, parent, sep_rhs, sep_inverse, sep_coupling))
    root_update = jnp.einsum('lwv,lvc->wc', root_coupling, sep_solution[:, SEPS - 1], precision=highest)
    root_residual = root_rhs - root_update
    root_solution = jnp.dot(root_inverse, root_residual, precision=highest)
    return sep_solution, root_solution
```

```python
import functools

import jax
import jax.numpy as jnp
from jax import lax
from jax.experimental import pallas as pl
from jax.experimental.pallas import tpu as pltpu
from jax.sharding import Mesh, PartitionSpec as P

ROW = ("xl", "xh", "y", "c")
NT = (((1,), (1,)), ((), ()))


def split(a):
    high = a.astype(jnp.bfloat16)
    return high, (a - high.astype(jnp.float32)).astype(jnp.bfloat16)


def dot3(a, b, dims):
    mm = functools.partial(lax.dot_general, dimension_numbers=dims, preferred_element_type=jnp.float32)
    return mm(a[0], b[0]) + (mm(a[0], b[1]) + mm(a[1], b[0]))


def leaf_kernel(meta, rhs, inv, coupling, sep, out, xt_hi, xt_lo, place):
    step = pl.program_id(0)
    parent, core, block = meta[0], meta[1], meta[2]
    k = 2 * (step % 2) + jnp.where(step < 2, 1 - core, core)

    @pl.when(step == 0)
    def _():
        x = dot3(split(inv[0, 0]), split(rhs[0, 0]), (((1,), (0,)), ((), ())))
        xt_hi[...], xt_lo[...] = split(x.T)
        place[...] = jnp.zeros_like(place)

    keep = jnp.where(k >= parent, 1.0, 0.0)
    got = dot3((xt_hi[...], xt_lo[...]), split(coupling[0, 0, 0]), NT)
    half = got.shape[0] // 2
    out[0, 0, 0] = got[:half] * -keep
    out[0, 1, 0] = got[half:] * -keep
    place[pl.ds(pl.multiple_of(8 * (block % 16), 8), 8), :] = sep[0, 0]
    lanes = pl.ds(pl.multiple_of(128 * (block // 16), 128), 128)
    own = place[...].T
    out[0, 0, 0, :, lanes] += own[:half]
    out[0, 1, 0, :, lanes] += own[half:]


def leaves(meta, rhs, inv, coupling, sep):
    n, width = coupling.shape[2], coupling.shape[3]
    leaf, cols = rhs.shape[2], rhs.shape[3]

    def level(s, m):
        return 2 * (s % 2) + jnp.where(s < 2, 1 - m[1], m[1])

    return pl.pallas_call(
        leaf_kernel,
        grid_spec=pltpu.PrefetchScalarGridSpec(
            num_scalar_prefetch=1,
            grid=(n,),
            in_specs=[
                pl.BlockSpec((1, 1, leaf, cols), lambda s, m: (0, 0, 0, 0)),
                pl.BlockSpec((1, 1, leaf, leaf), lambda s, m: (0, 0, 0, 0)),
                pl.BlockSpec((1, 1, 1, width, leaf), lambda s, m: (0, 0, level(s, m), 0, 0)),
                pl.BlockSpec((1, 1, 8, cols), lambda s, m: (0, level(s, m), 0, 0)),
            ],
            out_specs=pl.BlockSpec((1, 2, 1, cols // 2, width), lambda s, m: (s // 2, 0, s % 2, 0, 0)),
            scratch_shapes=[
                pltpu.VMEM((cols, leaf), jnp.bfloat16),
                pltpu.VMEM((cols, leaf), jnp.bfloat16),
                pltpu.VMEM((128, cols), jnp.float32),
            ],
        ),
        out_shape=jax.ShapeDtypeStruct((2, 2, 2, cols // 2, width), jnp.float32),
        compiler_params=pltpu.CompilerParams(vmem_limit_bytes=24 * 2**20),
        name="leaves",
    )(meta, rhs, inv, coupling, sep)


def body(
    leaf_rhs,
    leaf_inverse,
    leaf_coupling,
    parent,
    sep_rhs,
    sep_inverse,
    sep_coupling,
    root_coupling,
    root_rhs,
    root_inverse,
):
    layer = lax.axis_index("layer")
    xh, c = lax.axis_index("xh"), lax.axis_index("c")
    xl, y = lax.axis_index("xl"), lax.axis_index("y")
    width, cols = leaf_coupling.shape[3], leaf_rhs.shape[3]
    part = cols // 16

    rr = jnp.pad(root_rhs, ((0, 0), (0, width - cols)))
    table = [
        [sep_inverse[0, 0], root_coupling[0], root_inverse],
        [sep_inverse[0, 1], sep_coupling[0, 0], rr],
        [sep_inverse[0, 2], sep_coupling[0, 1], rr],
        [sep_inverse[0, 3], sep_coupling[0, 2], rr],
    ]
    for_core = [jnp.stack([jnp.stack(table[2 * h + k]) for h in range(2)]) for k in range(2)]
    keep = jnp.where(c == 0, for_core[0], for_core[1])
    send = jnp.where(c == 0, for_core[1], for_core[0])
    came = lax.ppermute(send, "c", [(0, 1), (1, 0)])
    both = jnp.stack([jnp.where(c == 0, keep, came), jnp.where(c == 0, came, keep)], axis=2)
    keep = jnp.where(xh == 0, both[0], both[1])
    send = jnp.where(xh == 0, both[1], both[0])
    came = lax.ppermute(send, "xh", [(0, 1), (1, 0)])
    mine = jnp.stack([jnp.where(xh == 0, keep, came), jnp.where(xh == 0, came, keep)], axis=1)
    full = lax.all_gather(mine, ("xl", "y"), axis=0, tiled=False)
    full = full.reshape(2, 8, 3, 2, 16, width).transpose(2, 0, 3, 1, 4, 5).reshape(3, width, width)

    block = lax.axis_index(ROW)
    meta = jnp.stack([parent[0, 0], c, block]).astype(jnp.int32)
    update = leaves(meta, leaf_rhs, leaf_inverse, leaf_coupling, sep_rhs)
    res = update[1] + lax.ppermute(update[0], "c", [(0, 1), (1, 0)])
    res = res.reshape(4, cols // 2, width)
    res = lax.all_to_all(res, ("xl", "xh"), 0, 0).sum(0)
    res = res.reshape(8, part, width)
    res = lax.all_to_all(res, "y", 0, 0).sum(0)

    mm = functools.partial(lax.dot_general, dimension_numbers=NT, precision=lax.Precision.HIGH)
    hop = functools.partial(lax.ppermute, axis_name=("xh", "c"))
    rr_own = lax.dynamic_slice_in_dim(full[2], (xl * 8 + y) * part, part, 1).T
    rr_cols = hop(rr_own, perm=[(1, 0)]) * jnp.where(layer == 0, 1.0, 0.0)
    sol = mm(res, full[0])
    for k in range(3):
        sol = sol - mm(hop(sol, perm=[(k, k + 1)]), full[1])
    term = mm(rr_cols - mm(hop(sol, perm=[(3, 0)]), full[1]), full[2])

    out = jnp.concatenate([sol.T.reshape(64, 8, part), term.T.reshape(64, 8, part)], axis=2)
    out = lax.all_to_all(out, ROW, 0, 0).reshape(2, 2, 8, 2, 8, 2, part)
    out = out.transpose(1, 3, 5, 4, 0, 2, 6).reshape(4, 2, 8, cols)
    sep_out = out[:, 0][None]
    term = jnp.broadcast_to(out[0, 1][None], (8, 8, cols))
    root_out = lax.all_to_all(term, "layer", 0, 0).sum(0)
    return (sep_out, root_out)


def solution(mesh):
    layers, rows = mesh.devices.shape
    fine = Mesh(mesh.devices.reshape(layers, 2, 2, 8, 2), ("layer",) + ROW)
    return jax.shard_map(
        body,
        mesh=fine,
        in_specs=(
            P("layer", ROW, None, None),
            P("layer", ROW, None, None),
            P("layer", ROW, None, None, None),
            P("layer", ROW),
            P("layer", None, ROW, None),
            P("layer", None, ROW, None),
            P("layer", None, ROW, None),
            P("layer", ROW, None),
            P(ROW, None),
            P(ROW, None),
        ),
        out_specs=(P("layer", None, ROW, None), P(ROW, None)),
        check_vma=False,
    )
```

```python
import functools

import jax
import jax.numpy as jnp
from jax import lax
from jax.experimental import pallas as pl
from jax.experimental.pallas import tpu as pltpu
from jax.sharding import Mesh, PartitionSpec as P

ROW = ("x", "y", "c")
NX, NY, NC = 4, 8, 2
NT = (((1,), (1,)), ((), ()))
NN = (((1,), (0,)), ((), ()))
VMEM = pl.BlockSpec(memory_space=pltpu.VMEM)


def split(a):
    high = a.astype(jnp.bfloat16)
    return high, (a - high.astype(jnp.float32)).astype(jnp.bfloat16)


def dot3(a, b, dims):
    mm = functools.partial(lax.dot_general, dimension_numbers=dims, preferred_element_type=jnp.float32)
    return mm(a[0], b[0]) + (mm(a[0], b[1]) + mm(a[1], b[0]))


def by_tiles(ref, part):
    tiles, rows, _ = ref.shape

    def column(tile):
        return jnp.concatenate(
            [
                ref[tile, pl.ds(base + t, 8, stride=part), :]
                for base in range(0, rows, 8 * part)
                for t in range(part)
            ],
            axis=0,
        )

    return jnp.concatenate([column(tile) for tile in range(tiles)], axis=1)


def leaf_kernel(part, meta, rhs, inv, coupling, sep, out, xt, xt_hi, xt_lo, place, own):
    k = pl.program_id(0)
    parent, core, block = meta[0], meta[1], meta[2]

    @pl.when(k == 0)
    def _():
        solved = dot3(split(inv[0, 0]), split(rhs[0, 0]), NN).T
        for tile in range(xt.shape[0]):
            xt[tile] = solved[:, 128 * tile : 128 * (tile + 1)]
        xt_hi[...], xt_lo[...] = split(by_tiles(xt, part))
        place[...] = jnp.zeros_like(place)

    keep = jnp.where(k >= parent, 1.0, 0.0)
    got = dot3((xt_hi[...], xt_lo[...]), split(coupling[0, 0, 0]), NT) * -keep
    place[pl.ds(pl.multiple_of(8 * (block % 16), 8), 8), :] = sep[0, 0]
    own[0] = place[...].T
    mine = by_tiles(own, part)
    group = 8 * part
    for half in range(NC):
        slot = jnp.where(core == half, 1, 0)
        for x in range(NX):
            rows = slice((half * NX + x) * group, (half * NX + x + 1) * group)
            for tile in range(out.shape[3]):
                out[slot, x, 0, tile] = got[rows, 128 * tile : 128 * (tile + 1)]
            out[slot, x, 0, block // 16] += mine[rows]


def leaves(meta, rhs, inv, coupling, sep):
    n, width = coupling.shape[2], coupling.shape[3]
    leaf, cols = rhs.shape[2], rhs.shape[3]
    part = cols // 64
    return pl.pallas_call(
        functools.partial(leaf_kernel, part),
        grid_spec=pltpu.PrefetchScalarGridSpec(
            num_scalar_prefetch=1,
            grid=(n,),
            in_specs=[
                pl.BlockSpec((1, 1, leaf, cols), lambda k, m: (0, 0, 0, 0)),
                pl.BlockSpec((1, 1, leaf, leaf), lambda k, m: (0, 0, 0, 0)),
                pl.BlockSpec((1, 1, 1, width, leaf), lambda k, m: (0, 0, k, 0, 0)),
                pl.BlockSpec((1, 1, 8, cols), lambda k, m: (0, k, 0, 0)),
            ],
            out_specs=pl.BlockSpec(
                (NC, NX, 1, width // 128, 8 * part, 128), lambda k, m: (0, 0, k, 0, 0, 0)
            ),
            scratch_shapes=[
                pltpu.VMEM((leaf // 128, cols, 128), jnp.float32),
                pltpu.VMEM((cols, leaf), jnp.bfloat16),
                pltpu.VMEM((cols, leaf), jnp.bfloat16),
                pltpu.VMEM((128, cols), jnp.float32),
                pltpu.VMEM((1, cols, 128), jnp.float32),
            ],
        ),
        out_shape=jax.ShapeDtypeStruct((NC, NX, n, width // 128, 8 * part, 128), jnp.float32),
        compiler_params=pltpu.CompilerParams(vmem_limit_bytes=24 * 2**20),
        name="leaves",
    )(meta, rhs, inv, coupling, sep)


def sum_kernel(parts, out):
    count = out.shape[1]
    for s in range(8):
        rows = pl.ds(s, count, stride=8)
        out[s] = (parts[0, rows, :] + parts[1, rows, :]) + (parts[2, rows, :] + parts[3, rows, :])


def chain_kernel(part, meta, parts, root_inverse, weights, out, own, full, wide, sems):
    x = meta[0]
    n = full.shape[0]
    copies = []
    for m in range(n):
        copies.append([])
        for back in range(NX):
            rows = pl.multiple_of(((x + NX - back) % NX) * 16, 16)
            copy = pltpu.make_async_copy(
                weights.at[:, back, m], full.at[m, pl.ds(rows, 16)], sems.at[m, back]
            )
            copy.start()
            copies[-1].append(copy)

    def matrix(m):
        for copy in copies[m]:
            copy.wait()
        return full[m].reshape(full.shape[1] * 8, full.shape[3])

    res = parts[0]
    for p in range(1, parts.shape[0]):
        res = res + parts[p]
    tiles = res.shape[0] // (4 * part)

    def residual(k):
        starts = [part * (tiles * k + tile) for tile in range(tiles)]
        return jnp.concatenate([res[at : at + part] for at in starts], axis=1)

    wide[...] = jnp.zeros_like(wide)
    sol = None
    for k in range(4):
        now = dot3(split(residual(k)), split(matrix(k)), NT)
        if k > 0:
            now = now - dot3(split(sol), split(matrix(3 + k)), NT)
        sol = now
        wide[part * k : part * (k + 1), :] = sol
    term = dot3(split(sol), split(matrix(7)), NT)
    wide[4 * part : 5 * part, :] = dot3(split(term), split(matrix(8)), NT)
    back = wide[...].T
    out[...] = back.reshape(out.shape)
    own[...] = dot3(split(root_inverse[...]), split(matrix(9)), NN)[:, : own.shape[1]]


def body(
    leaf_rhs,
    leaf_inverse,
    leaf_coupling,
    parent,
    sep_rhs,
    sep_inverse,
    sep_coupling,
    root_coupling,
    root_rhs,
    root_inverse,
):
    x, c = lax.axis_index("x"), lax.axis_index("c")
    width, cols = leaf_coupling.shape[3], leaf_rhs.shape[3]
    part = cols // 64

    pack = jnp.concatenate(
        [
            sep_inverse[0],
            sep_coupling[0],
            root_coupling,
            root_inverse[None],
            jnp.pad(root_rhs, ((0, 0), (0, width - cols)))[None],
        ]
    )
    ring = [pack] + [
        lax.ppermute(pack, "x", [(i, (i + j) % NX) for i in range(NX)]) for j in range(1, NX)
    ]
    weights = lax.all_gather(jnp.stack(ring), ("y", "c"))

    meta = jnp.stack([parent[0, 0], c, lax.axis_index(ROW)]).astype(jnp.int32)
    update = leaves(meta, leaf_rhs, leaf_inverse, leaf_coupling, sep_rhs)
    res = update[1] + lax.ppermute(update[0], "c", [(0, 1), (1, 0)])
    tall = width // 128 * part
    res = lax.all_to_all(res.reshape(NX, 4 * 8 * tall, 128), "x", 0, 0)
    res = pl.pallas_call(
        sum_kernel,
        in_specs=[VMEM],
        out_specs=VMEM,
        out_shape=jax.ShapeDtypeStruct((8, 4 * tall, 128), jnp.float32),
        compiler_params=pltpu.CompilerParams(vmem_limit_bytes=16 * 2**20),
        name="sum_x",
    )(res)
    res = lax.all_to_all(res, "y", 0, 0)

    out, own = pl.pallas_call(
        functools.partial(chain_kernel, part),
        in_specs=[pl.BlockSpec(memory_space=pltpu.SMEM), VMEM, VMEM, pl.BlockSpec(memory_space=pl.ANY)],
        out_specs=[VMEM, VMEM],
        out_shape=[
            jax.ShapeDtypeStruct((64, 8, 128), jnp.float32),
            jax.ShapeDtypeStruct((8, cols), jnp.float32),
        ],
        scratch_shapes=[
            pltpu.VMEM((10, 64, 8, width), jnp.float32),
            pltpu.VMEM((128, width), jnp.float32),
            pltpu.SemaphoreType.DMA((10, NX)),
        ],
        compiler_params=pltpu.CompilerParams(vmem_limit_bytes=40 * 2**20),
        name="chain",
    )(x.reshape(1).astype(jnp.int32), res, root_inverse, weights)

    out = lax.all_to_all(out, ROW, 0, 0)[:, :, : 5 * part]
    out = out.reshape(NX, NY, NC, 8, 5, part).transpose(4, 3, 2, 0, 1, 5).reshape(5, 8, cols)
    term = jnp.broadcast_to(out[4][None], (8, 8, cols))
    root_out = own - lax.all_to_all(term, "layer", 0, 0).sum(0)
    return (out[:4][None], root_out)


def solution(mesh):
    fine = Mesh(mesh.devices.reshape(-1, NX, NY, NC), ("layer",) + ROW)
    return jax.shard_map(
        body,
        mesh=fine,
        in_specs=(
            P("layer", ROW, None, None),
            P("layer", ROW, None, None),
            P("layer", ROW, None, None, None),
            P("layer", ROW),
            P("layer", None, ROW, None),
            P("layer", None, ROW, None),
            P("layer", None, ROW, None),
            P("layer", ROW, None),
            P(ROW, None),
            P(ROW, None),
        ),
        out_specs=(P("layer", None, ROW, None), P(ROW, None)),
        check_vma=False,
    )
```

```python
import functools

import jax
import jax.numpy as jnp
from jax import lax
from jax.experimental import pallas as pl
from jax.experimental.pallas import tpu as pltpu
from jax.sharding import Mesh, PartitionSpec as P

ROW = ("xl", "xh", "y", "c")
X = ("xl", "xh")
NX, NY, NC = 4, 8, 2
NT = (((1,), (1,)), ((), ()))
NN = (((1,), (0,)), ((), ()))
VMEM = pl.BlockSpec(memory_space=pltpu.VMEM)
SMEM = pl.BlockSpec(memory_space=pltpu.SMEM)
HBM = pl.BlockSpec(memory_space=pltpu.HBM)
FLAT = jax.ShapeDtypeStruct


def split(a):
    high = a.astype(jnp.bfloat16)
    return high, (a - high.astype(jnp.float32)).astype(jnp.bfloat16)


def dot3(a, b, dims):
    mm = functools.partial(lax.dot_general, dimension_numbers=dims, preferred_element_type=jnp.float32)
    return mm(a[0], b[0]) + (mm(a[0], b[1]) + mm(a[1], b[0]))


def by_tiles(ref, part):
    tiles, rows, _ = ref.shape

    def column(tile):
        return jnp.concatenate(
            [
                ref[tile, pl.ds(base + t, 8, stride=part), :]
                for base in range(0, rows, 8 * part)
                for t in range(part)
            ],
            axis=0,
        )

    return jnp.concatenate([column(tile) for tile in range(tiles)], axis=1)


def pack_kernel(meta, sep_inverse, sep_coupling, root_coupling, root_rhs, root_inverse, same, other):
    zeros = jnp.zeros_like(root_inverse)
    rr = jnp.concatenate([root_rhs[...], zeros[:, root_rhs.shape[1] :]], axis=1)
    tables = (
        [sep_inverse[0, 0], sep_inverse[0, 1], sep_coupling[0, 0], rr, zeros, zeros],
        [
            sep_inverse[0, 2],
            sep_inverse[0, 3],
            sep_coupling[0, 1],
            sep_coupling[0, 2],
            root_coupling[0],
            root_inverse[...],
        ],
    )
    for side in range(2):

        @pl.when(meta[0] == side)
        def _():
            for m in range(same.shape[0]):
                same[m] = tables[side][m]
                other[m] = tables[1 - side][m]


def leaf_kernel(part, meta, rhs, inv, coupling, sep, out, xt, xt_hi, xt_lo, place, own):
    k = pl.program_id(0)
    parent, core, block = meta[0], meta[1], meta[2]

    @pl.when(k == 0)
    def _():
        solved = dot3(split(inv[0, 0]), split(rhs[0, 0]), NN).T
        for tile in range(xt.shape[0]):
            xt[tile] = solved[:, 128 * tile : 128 * (tile + 1)]
        xt_hi[...], xt_lo[...] = split(by_tiles(xt, part))
        place[...] = jnp.zeros_like(place)

    keep = jnp.where(k >= parent, 1.0, 0.0)
    got = dot3((xt_hi[...], xt_lo[...]), split(coupling[0, 0, 0]), NT) * -keep
    place[pl.ds(pl.multiple_of(8 * (block % 16), 8), 8), :] = sep[0, 0]
    own[0] = place[...].T
    mine = by_tiles(own, part)
    group = 8 * part
    for half in range(NC):
        slot = jnp.where(core == half, 1, 0)
        for side in range(2):
            rows = slice((half * 2 + side) * group, (half * 2 + side + 1) * group)
            for tile in range(out.shape[4]):
                out[slot, side, 0, 0, tile] = got[rows, 128 * tile : 128 * (tile + 1)]
            out[slot, side, 0, 0, block // 16] += mine[rows]


def leaves(meta, rhs, inv, coupling, sep):
    n, width = coupling.shape[2], coupling.shape[3]
    leaf, cols = rhs.shape[2], rhs.shape[3]
    part = cols // 32
    return pl.pallas_call(
        functools.partial(leaf_kernel, part),
        grid_spec=pltpu.PrefetchScalarGridSpec(
            num_scalar_prefetch=1,
            grid=(n,),
            in_specs=[
                pl.BlockSpec((1, 1, leaf, cols), lambda k, m: (0, 0, 0, 0)),
                pl.BlockSpec((1, 1, leaf, leaf), lambda k, m: (0, 0, 0, 0)),
                pl.BlockSpec((1, 1, 1, width, leaf), lambda k, m: (0, 0, k, 0, 0)),
                pl.BlockSpec((1, 1, 8, cols), lambda k, m: (0, k, 0, 0)),
            ],
            out_specs=pl.BlockSpec(
                (NC, 2, 1, 1, width // 128, 8 * part, 128),
                lambda k, m: (0, 0, k // 2, k % 2, 0, 0, 0),
            ),
            scratch_shapes=[
                pltpu.VMEM((leaf // 128, cols, 128), jnp.float32),
                pltpu.VMEM((cols, leaf), jnp.bfloat16),
                pltpu.VMEM((cols, leaf), jnp.bfloat16),
                pltpu.VMEM((128, cols), jnp.float32),
                pltpu.VMEM((1, cols, 128), jnp.float32),
            ],
        ),
        out_shape=FLAT((NC, 2, 2, 2, width // 128, 8 * part, 128), jnp.float32),
        compiler_params=pltpu.CompilerParams(vmem_limit_bytes=24 * 2**20),
        name="leaves",
    )(meta, rhs, inv, coupling, sep)


def sum_kernel(parts, out):
    count = out.shape[1]
    for s in range(8):
        rows = pl.ds(s, count, stride=8)
        out[s] = (parts[0, rows, :] + parts[1, rows, :]) + (parts[2, rows, :] + parts[3, rows, :])


def fetch(weights, full, sems, x, slots):
    copies = {}
    for at, m in enumerate(slots):
        copies[m] = []
        for back in range(NX):
            rows = pl.multiple_of(((x + NX - back) % NX) * 16, 16)
            copy = pltpu.make_async_copy(
                weights.at[:, back, m], full.at[at, pl.ds(rows, 16)], sems.at[at, back]
            )
            copy.start()
            copies[m].append(copy)

    def matrix(m):
        for copy in copies[m]:
            copy.wait()
        block = full[slots.index(m)]
        return split(block.reshape(-1, block.shape[-1]))

    return matrix


def first_kernel(part, meta, parts, weights, held, send, full, sems):
    matrix = fetch(weights, full, sems, meta[0], [0, 1, 2, 3])
    res = parts[0]
    for p in range(1, parts.shape[0]):
        res = res + parts[p]
    tiles = res.shape[0] // (2 * part)

    def residual(k):
        starts = [part * (tiles * k + tile) for tile in range(tiles)]
        return split(jnp.concatenate([res[at : at + part] for at in starts], axis=1))

    wide = held.shape[2]
    first = dot3(residual(0), matrix(0), NT)
    second = dot3(residual(1), matrix(1), NT)
    chained = second - dot3(split(first), matrix(2), NT)
    shape = (part, wide)
    mine = lax.broadcasted_iota(jnp.int32, shape, 1) == lax.broadcasted_iota(jnp.int32, shape, 0) + part * meta[1]
    pick = jnp.where(mine, jnp.where(meta[2] == 0, 1.0, 0.0), 0.0).astype(jnp.bfloat16)
    high, low = matrix(3)
    mm = functools.partial(lax.dot_general, dimension_numbers=NT, preferred_element_type=jnp.float32)
    held[0] = first
    held[1] = jnp.where(meta[0] % 2 == 0, chained, second)
    send[0] = chained
    send[1] = mm(pick, high) + mm(pick, low)


def second_kernel(part, meta, held, came, weights, out, full, wide, sems):
    wide[...] = jnp.zeros_like(wide)

    @pl.when(meta[0] % 2 == 0)
    def _():
        wide[:part, :] = held[0]
        wide[part : 2 * part, :] = held[1]

    @pl.when(meta[0] % 2 == 1)
    def _():
        matrix = fetch(weights, full, sems, meta[0], [2, 3, 4, 5])
        third = held[0] - dot3(split(came[0]), matrix(2), NT)
        wide[:part, :] = third
        fourth = held[1] - dot3(split(third), matrix(3), NT)
        wide[part : 2 * part, :] = fourth
        term = came[1] - dot3(split(fourth), matrix(4), NT)
        wide[2 * part : 3 * part, :] = dot3(split(term), matrix(5), NT)

    back = wide[...].T
    out[...] = back.reshape(out.shape)


def body(
    leaf_rhs,
    leaf_inverse,
    leaf_coupling,
    parent,
    sep_rhs,
    sep_inverse,
    sep_coupling,
    root_coupling,
    root_rhs,
    root_inverse,
):
    xl, xh = lax.axis_index("xl"), lax.axis_index("xh")
    y, c, layer = lax.axis_index("y"), lax.axis_index("c"), lax.axis_index("layer")
    width, cols = leaf_coupling.shape[3], leaf_rhs.shape[3]
    part = cols // 32
    tiles = width // 128
    call = pl.pallas_call

    same, other = call(
        pack_kernel,
        in_specs=[SMEM] + [VMEM] * 5,
        out_specs=[VMEM, VMEM],
        out_shape=[FLAT((6, 8, width), jnp.float32)] * 2,
        name="pack",
    )(xh.reshape(1).astype(jnp.int32), sep_inverse, sep_coupling, root_coupling, root_rhs, root_inverse)
    ring = [same] + [
        lax.ppermute(pack, X, [(i, (i + j) % NX) for i in range(NX)])
        for j, pack in ((1, other), (2, same), (3, other))
    ]

    meta = jnp.stack([parent[0, 0], c, lax.axis_index(ROW)]).astype(jnp.int32)
    update = leaves(meta, leaf_rhs, leaf_inverse, leaf_coupling, sep_rhs)
    ring, update = lax.optimization_barrier((ring, update))
    weights = lax.all_gather(jnp.stack(ring), ("y", "c"))
    res = update[1] + lax.ppermute(update[0], "c", [(0, 1), (1, 0)])
    res = lax.all_to_all(res.reshape(NX, 2 * tiles * 8 * part, 128), X, 0, 0)
    res = call(
        sum_kernel,
        in_specs=[VMEM],
        out_specs=VMEM,
        out_shape=FLAT((8, 2 * tiles * part, 128), jnp.float32),
        compiler_params=pltpu.CompilerParams(vmem_limit_bytes=16 * 2**20),
        name="sum_x",
    )(res)
    res = lax.all_to_all(res, "y", 0, 0)

    meta = jnp.stack([2 * xl + xh, (c * 2 + xl) * NY + y, layer]).astype(jnp.int32)
    scratch = [pltpu.VMEM((4, 64, 8, width), jnp.float32)]
    sems = [pltpu.SemaphoreType.DMA((4, NX))]
    params = pltpu.CompilerParams(vmem_limit_bytes=32 * 2**20)
    held, send = call(
        functools.partial(first_kernel, part),
        in_specs=[SMEM, VMEM, HBM],
        out_specs=[VMEM, VMEM],
        out_shape=[FLAT((2, part, width), jnp.float32)] * 2,
        scratch_shapes=scratch + sems,
        compiler_params=params,
        name="chain_first",
    )(meta, res, weights)
    came = lax.ppermute(send, "xh", [(0, 1)])
    out = call(
        functools.partial(second_kernel, part),
        in_specs=[SMEM, VMEM, VMEM, HBM],
        out_specs=VMEM,
        out_shape=FLAT((64, 8, 128), jnp.float32),
        scratch_shapes=scratch + [pltpu.VMEM((128, width), jnp.float32)] + sems,
        compiler_params=params,
        name="chain_second",
    )(meta, held, came, weights)

    out = lax.all_to_all(out, ROW, 0, 0)[:, :, : 3 * part]
    out = out.reshape(2, 2, NY, NC, 8, 3, part).transpose(1, 5, 4, 3, 0, 2, 6).reshape(2, 3, 8, cols)
    term = jnp.broadcast_to(out[1, 2][None], (8, 8, cols))
    root_out = lax.all_to_all(term, "layer", 0, 0).sum(0)
    return (out[:, :2].reshape(1, 4, 8, cols), root_out)


def solution(mesh):
    fine = Mesh(mesh.devices.reshape(-1, 2, 2, NY, NC), ("layer",) + ROW)
    return jax.shard_map(
        body,
        mesh=fine,
        in_specs=(
            P("layer", ROW, None, None),
            P("layer", ROW, None, None),
            P("layer", ROW, None, None, None),
            P("layer", ROW),
            P("layer", None, ROW, None),
            P("layer", None, ROW, None),
            P("layer", None, ROW, None),
            P("layer", ROW, None),
            P(ROW, None),
            P(ROW, None),
        ),
        out_specs=(P("layer", None, ROW, None), P(ROW, None)),
        check_vma=False,
    )
```

```python
import functools

import jax
import jax.numpy as jnp
from jax import lax
from jax.experimental import pallas as pl
from jax.experimental.pallas import tpu as pltpu
from jax.sharding import Mesh, PartitionSpec as P

ROW = ("xl", "xh", "y", "c")
X = ("xl", "xh")
NX, NY, NC = 4, 8, 2
NT = (((1,), (1,)), ((), ()))
NN = (((1,), (0,)), ((), ()))
VMEM = pl.BlockSpec(memory_space=pltpu.VMEM)
SMEM = pl.BlockSpec(memory_space=pltpu.SMEM)
HBM = pl.BlockSpec(memory_space=pltpu.HBM)
FLAT = jax.ShapeDtypeStruct


def split(a):
    high = a.astype(jnp.bfloat16)
    return high, (a - high.astype(jnp.float32)).astype(jnp.bfloat16)


def dot3(a, b, dims):
    mm = functools.partial(lax.dot_general, dimension_numbers=dims, preferred_element_type=jnp.float32)
    return mm(a[0], b[0]) + (mm(a[0], b[1]) + mm(a[1], b[0]))


def by_tiles(ref, part):
    tiles, rows, _ = ref.shape

    def column(tile):
        return jnp.concatenate(
            [
                ref[tile, pl.ds(base + t, 8, stride=part), :]
                for base in range(0, rows, 8 * part)
                for t in range(part)
            ],
            axis=0,
        )

    return jnp.concatenate([column(tile) for tile in range(tiles)], axis=1)


def pack_kernel(meta, sep_inverse, sep_coupling, root_coupling, root_rhs, root_inverse, same, other):
    zeros = jnp.zeros_like(root_inverse)
    rr = jnp.concatenate([root_rhs[...], zeros[:, root_rhs.shape[1] :]], axis=1)
    tables = (
        [sep_inverse[0, 0], sep_inverse[0, 1], sep_coupling[0, 0], rr, zeros, zeros],
        [
            sep_inverse[0, 2],
            sep_inverse[0, 3],
            sep_coupling[0, 1],
            sep_coupling[0, 2],
            root_coupling[0],
            root_inverse[...],
        ],
    )
    for side in range(2):

        @pl.when(meta[0] == side)
        def _():
            for m in range(same.shape[0]):
                same[m] = tables[side][m]
                other[m] = tables[1 - side][m]


def leaf_kernel(part, meta, rhs, inv, coupling, sep, out, xt, xt_hi, xt_lo, place, own):
    k = pl.program_id(0)
    parent, core, block = meta[0], meta[1], meta[2]

    @pl.when(k == 0)
    def _():
        solved = dot3(split(inv[0, 0]), split(rhs[0, 0]), NN).T
        for tile in range(xt.shape[0]):
            xt[tile] = solved[:, 128 * tile : 128 * (tile + 1)]
        xt_hi[...], xt_lo[...] = split(by_tiles(xt, part))
        place[...] = jnp.zeros_like(place)

    keep = jnp.where(k >= parent, 1.0, 0.0)
    got = dot3((xt_hi[...], xt_lo[...]), split(coupling[0, 0, 0]), NT) * -keep
    place[pl.ds(pl.multiple_of(8 * (block % 16), 8), 8), :] = sep[0, 0]
    own[0] = place[...].T
    mine = by_tiles(own, part)
    group = 8 * part
    for half in range(NC):
        slot = jnp.where(core == half, 1, 0)
        for side in range(2):
            rows = slice((half * 2 + side) * group, (half * 2 + side + 1) * group)
            for tile in range(out.shape[4]):
                out[slot, side, 0, 0, tile] = got[rows, 128 * tile : 128 * (tile + 1)]
            out[slot, side, 0, 0, block // 16] += mine[rows]


def leaves(meta, rhs, inv, coupling, sep):
    n, width = coupling.shape[2], coupling.shape[3]
    leaf, cols = rhs.shape[2], rhs.shape[3]
    part = cols // 32
    return pl.pallas_call(
        functools.partial(leaf_kernel, part),
        grid_spec=pltpu.PrefetchScalarGridSpec(
            num_scalar_prefetch=1,
            grid=(n,),
            in_specs=[
                pl.BlockSpec((1, 1, leaf, cols), lambda k, m: (0, 0, 0, 0)),
                pl.BlockSpec((1, 1, leaf, leaf), lambda k, m: (0, 0, 0, 0)),
                pl.BlockSpec((1, 1, 1, width, leaf), lambda k, m: (0, 0, k, 0, 0)),
                pl.BlockSpec((1, 1, 8, cols), lambda k, m: (0, k, 0, 0)),
            ],
            out_specs=pl.BlockSpec(
                (NC, 2, 1, 1, width // 128, 8 * part, 128),
                lambda k, m: (0, 0, k // 2, k % 2, 0, 0, 0),
            ),
            scratch_shapes=[
                pltpu.VMEM((leaf // 128, cols, 128), jnp.float32),
                pltpu.VMEM((cols, leaf), jnp.bfloat16),
                pltpu.VMEM((cols, leaf), jnp.bfloat16),
                pltpu.VMEM((128, cols), jnp.float32),
                pltpu.VMEM((1, cols, 128), jnp.float32),
            ],
        ),
        out_shape=FLAT((NC, 2, 2, 2, width // 128, 8 * part, 128), jnp.float32),
        compiler_params=pltpu.CompilerParams(vmem_limit_bytes=24 * 2**20),
        name="leaves",
    )(meta, rhs, inv, coupling, sep)


def sum_kernel(parts, out):
    count = out.shape[1]
    for s in range(8):
        rows = pl.ds(s, count, stride=8)
        out[s] = (parts[0, rows, :] + parts[1, rows, :]) + (parts[2, rows, :] + parts[3, rows, :])


def first_kernel(part, meta, parts, weights, held, send, high, low, full, sems):
    x = meta[0]
    copies = []
    for m in range(full.shape[0]):
        copies.append([])
        for back in range(NX):
            rows = pl.multiple_of(((x + NX - back) % NX) * 16, 16)
            copy = pltpu.make_async_copy(
                weights.at[:, back, m], full.at[m, pl.ds(rows, 16)], sems.at[m, back]
            )
            copy.start()
            copies[-1].append(copy)

    def matrix(m):
        for copy in copies[m]:
            copy.wait()
        return split(full[m].reshape(-1, full.shape[3]))

    res = parts[0]
    for p in range(1, parts.shape[0]):
        res = res + parts[p]
    tiles = res.shape[0] // (2 * part)

    def residual(k):
        starts = [part * (tiles * k + tile) for tile in range(tiles)]
        return split(jnp.concatenate([res[at : at + part] for at in starts], axis=1))

    first = dot3(residual(0), matrix(0), NT)
    second = dot3(residual(1), matrix(1), NT)
    held[0] = first
    held[1] = second
    last = [matrix(m) for m in range(2, full.shape[0])]

    @pl.when(x % 2 == 0)
    def _():
        chained = second - dot3(split(first), last[0], NT)
        shape = (part, held.shape[2])
        column = lax.broadcasted_iota(jnp.int32, shape, 0) + part * meta[1]
        mine = lax.broadcasted_iota(jnp.int32, shape, 1) == column
        pick = jnp.where(mine, jnp.where(meta[2] == 0, 1.0, 0.0), 0.0).astype(jnp.bfloat16)
        mm = functools.partial(lax.dot_general, dimension_numbers=NT, preferred_element_type=jnp.float32)
        held[1] = chained
        send[0] = chained
        send[1] = mm(pick, last[1][0]) + mm(pick, last[1][1])

    @pl.when(x % 2 == 1)
    def _():
        for at, pair in enumerate(last):
            high[at], low[at] = pair


def second_kernel(part, meta, held, came, high, low, out, wide):
    wide[...] = jnp.zeros_like(wide)
    step = 40

    def store(at, value):
        for copy in range(3):
            wide[step * copy + part * at : step * copy + part * (at + 1), :] = value

    @pl.when(meta[0] % 2 == 0)
    def _():
        store(0, held[0])
        store(1, held[1])

    @pl.when(meta[0] % 2 == 1)
    def _():
        third = held[0] - dot3(split(came[0]), (high[0], low[0]), NT)
        store(0, third)
        fourth = held[1] - dot3(split(third), (high[1], low[1]), NT)
        store(1, fourth)
        term = came[1] - dot3(split(fourth), (high[2], low[2]), NT)
        store(2, dot3(split(term), (high[3], low[3]), NT))

    rows = wide[...].T.reshape(-1, 8, 128)
    lane = lax.broadcasted_iota(jnp.int32, (rows.shape[0], 1, 128), 2)
    for j in range(3):
        far = min(6 + j, 7)
        low_rows = jnp.where(lane < 80, rows[:, 3 + j : 4 + j], rows[:, far : far + 1])
        out[:, j : j + 1, :] = jnp.where(lane < 40, rows[:, j : j + 1], low_rows)


def unpack_kernel(part, got, sep, term, tall):
    for src in range(got.shape[0]):
        tall[8 * src : 8 * src + 3, :] = got[src]
        tall[8 * src + 3 : 8 * src + 6, :] = got[src]
        tall[8 * src + 6 : 8 * src + 8, :] = got[src, 0:2]
    flat = tall[...]
    row = lax.broadcasted_iota(jnp.int32, flat.shape, 0) % 8
    flat = jnp.where(
        row < 3, flat, jnp.where(row < 6, pltpu.roll(flat, 128 - 40, 1), pltpu.roll(flat, 128 - 80, 1))
    )
    lane = lax.broadcasted_iota(jnp.int32, (8, 128), 1)
    tiles = sep.shape[3] // 128
    full = [[jnp.zeros((8, 128), jnp.float32) for _ in range(tiles)] for _ in range(5)]
    for src in range(got.shape[0]):
        xl, xh, y, c = src // 32, src // 16 % 2, src // 2 % 8, src % 2
        block = flat[8 * src : 8 * src + 8]
        start = part * ((c * 2 + xl) * NY + y)
        for at in range(2 + xh):
            moved = pltpu.roll(block, (start - part * at) % 128, 1)
            to = 2 * xh + at
            for tile in range(start // 128, (start + part - 1) // 128 + 1):
                at_lane = lane + 128 * tile
                here = (at_lane >= start) & (at_lane < start + part)
                full[to][tile] = jnp.where(here, moved, full[to][tile])
    for tile in range(tiles):
        lanes = slice(128 * tile, 128 * (tile + 1))
        for k in range(4):
            sep[0, k, :, lanes] = full[k][tile]
        for layer in range(term.shape[0]):
            term[layer, :, lanes] = full[4][tile]


def in_hbm(array):
    return pltpu.with_memory_space_constraint(array, pltpu.HBM)


def body(
    leaf_rhs,
    leaf_inverse,
    leaf_coupling,
    parent,
    sep_rhs,
    sep_inverse,
    sep_coupling,
    root_coupling,
    root_rhs,
    root_inverse,
):
    xl, xh = lax.axis_index("xl"), lax.axis_index("xh")
    y, c, layer = lax.axis_index("y"), lax.axis_index("c"), lax.axis_index("layer")
    width, cols = leaf_coupling.shape[3], leaf_rhs.shape[3]
    part = cols // 32
    tiles = width // 128
    call = pl.pallas_call

    same, other = call(
        pack_kernel,
        in_specs=[SMEM] + [VMEM] * 5,
        out_specs=[VMEM, VMEM],
        out_shape=[FLAT((6, 8, width), jnp.float32)] * 2,
        name="pack",
    )(xh.reshape(1).astype(jnp.int32), sep_inverse, sep_coupling, root_coupling, root_rhs, root_inverse)
    ring = [same] + [
        lax.ppermute(pack, X, [(i, (i + j) % NX) for i in range(NX)])
        for j, pack in ((1, other), (2, same), (3, other))
    ]

    meta = jnp.stack([parent[0, 0], c, lax.axis_index(ROW)]).astype(jnp.int32)
    update = leaves(meta, *map(in_hbm, (leaf_rhs, leaf_inverse, leaf_coupling, sep_rhs)))
    ring, update = lax.optimization_barrier((ring, update))
    weights = lax.all_gather(jnp.stack(ring), ("y", "c"))
    res = update[1] + lax.ppermute(update[0], "c", [(0, 1), (1, 0)])
    res = lax.all_to_all(res.reshape(NX, 2 * tiles * 8 * part, 128), X, 0, 0)
    res = call(
        sum_kernel,
        in_specs=[VMEM],
        out_specs=VMEM,
        out_shape=FLAT((8, 2 * tiles * part, 128), jnp.float32),
        compiler_params=pltpu.CompilerParams(vmem_limit_bytes=16 * 2**20),
        name="sum_x",
    )(res)
    res = lax.all_to_all(res, "y", 0, 0)

    meta = jnp.stack([2 * xl + xh, (c * 2 + xl) * NY + y, layer]).astype(jnp.int32)
    held, send, high, low = call(
        functools.partial(first_kernel, part),
        in_specs=[SMEM, VMEM, HBM],
        out_specs=[VMEM] * 4,
        out_shape=[FLAT((2, part, width), jnp.float32)] * 2 + [FLAT((4, width, width), jnp.bfloat16)] * 2,
        scratch_shapes=[pltpu.VMEM((6, 64, 8, width), jnp.float32), pltpu.SemaphoreType.DMA((6, NX))],
        compiler_params=pltpu.CompilerParams(vmem_limit_bytes=32 * 2**20),
        name="chain_first",
    )(meta, res, in_hbm(weights))
    came = lax.ppermute(send, "xh", [(0, 1)])
    out = call(
        functools.partial(second_kernel, part),
        in_specs=[SMEM] + [VMEM] * 4,
        out_specs=VMEM,
        out_shape=FLAT((64, 3, 128), jnp.float32),
        scratch_shapes=[pltpu.VMEM((128, width), jnp.float32)],
        compiler_params=pltpu.CompilerParams(vmem_limit_bytes=16 * 2**20),
        name="chain_second",
    )(meta, held, came, high, low)

    out = lax.all_to_all(out, ROW, 0, 0)
    sep_out, term = call(
        functools.partial(unpack_kernel, part),
        in_specs=[VMEM],
        out_specs=[VMEM] * 2,
        out_shape=[FLAT((1, 4, 8, cols), jnp.float32), FLAT((8, 8, cols), jnp.float32)],
        scratch_shapes=[pltpu.VMEM((64 * 8, 128), jnp.float32)],
        name="unpack",
    )(out)
    root_out = lax.all_to_all(term, "layer", 0, 0).sum(0)
    return (sep_out, root_out)


def solution(mesh):
    fine = Mesh(mesh.devices.reshape(-1, 2, 2, NY, NC), ("layer",) + ROW)
    return jax.shard_map(
        body,
        mesh=fine,
        in_specs=(
            P("layer", ROW, None, None),
            P("layer", ROW, None, None),
            P("layer", ROW, None, None, None),
            P("layer", ROW),
            P("layer", None, ROW, None),
            P("layer", None, ROW, None),
            P("layer", None, ROW, None),
            P("layer", ROW, None),
            P(ROW, None),
            P(ROW, None),
        ),
        out_specs=(P("layer", None, ROW, None), P(ROW, None)),
        check_vma=False,
    )
```

```python
import functools

import jax
import jax.numpy as jnp
from jax import lax
from jax.experimental import pallas as pl
from jax.experimental.pallas import tpu as pltpu
from jax.sharding import Mesh, PartitionSpec as P

ROW = ("xl", "xh", "y", "c")
X = ("xl", "xh")
NX, NY, NC = 4, 8, 2
NT = (((1,), (1,)), ((), ()))
NN = (((1,), (0,)), ((), ()))
VMEM = pl.BlockSpec(memory_space=pltpu.VMEM)
SMEM = pl.BlockSpec(memory_space=pltpu.SMEM)
HBM = pl.BlockSpec(memory_space=pltpu.HBM)
FLAT = jax.ShapeDtypeStruct


def split(a):
    high = a.astype(jnp.bfloat16)
    return high, (a - high.astype(jnp.float32)).astype(jnp.bfloat16)


def dot3(a, b, dims):
    mm = functools.partial(lax.dot_general, dimension_numbers=dims, preferred_element_type=jnp.float32)
    return mm(a[0], b[0]) + (mm(a[0], b[1]) + mm(a[1], b[0]))


def by_tiles(ref, part, base):
    tiles, rows, _ = ref.shape

    def column(tile):
        return jnp.concatenate(
            [
                ref[tile, pl.ds(base + block + t, 8, stride=part), :]
                for block in range(0, rows // NC, 8 * part)
                for t in range(part)
            ],
            axis=0,
        )

    return jnp.concatenate([column(tile) for tile in range(tiles)], axis=1)


def place():
    x = 2 * lax.axis_index("xl") + lax.axis_index("xh")
    return x, (x * NY + lax.axis_index("y")) * NC + lax.axis_index("c")


def pack_kernel(sep_inverse, sep_coupling, root_coupling, root_rhs, root_inverse, same, other):
    zeros = jnp.zeros_like(root_inverse)
    rr = jnp.concatenate([root_rhs[...], zeros[:, root_rhs.shape[1] :]], axis=1)
    tables = (
        [sep_inverse[0, 0], sep_inverse[0, 1], sep_coupling[0, 0], rr, zeros, zeros],
        [
            sep_inverse[0, 2],
            sep_inverse[0, 3],
            sep_coupling[0, 1],
            sep_coupling[0, 2],
            root_coupling[0],
            root_inverse[...],
        ],
    )
    for side in range(2):

        @pl.when(lax.axis_index("xh") == side)
        def _():
            for m in range(same.shape[0]):
                same[m] = tables[side][m]
                other[m] = tables[1 - side][m]


def half_update(part, other, parent, xt, coupling, sep, out, xt_hi, xt_lo, tall, own):
    k = pl.program_id(0)
    core = lax.axis_index("c")
    base = (1 - core if other else core) * (xt.shape[1] // NC)

    @pl.when(k == 0)
    def _():
        xt_hi[...], xt_lo[...] = split(by_tiles(xt, part, base))
        tall[...] = jnp.zeros_like(tall)

    keep = jnp.where(k >= parent[0, 0], 1.0, 0.0)
    got = dot3((xt_hi[...], xt_lo[...]), split(coupling[0, 0, 0]), NT) * -keep
    block = place()[1]
    tall[pl.ds(pl.multiple_of(8 * (block % 16), 8), 8), :] = sep[0, 0]
    own[0] = tall[...].T
    mine = by_tiles(own, part, base)
    group = 8 * part
    for side in range(2):
        rows = slice(side * group, (side + 1) * group)
        for tile in range(out.shape[3]):
            out[side, 0, 0, tile] = got[rows, 128 * tile : 128 * (tile + 1)]
        out[side, 0, 0, block // 16] += mine[rows]


def send_kernel(part, parent, rhs, inv, coupling, sep, out, xt, *scratch):
    @pl.when(pl.program_id(0) == 0)
    def _():
        solved = dot3(split(inv[0, 0]), split(rhs[0, 0]), NN).T
        for tile in range(xt.shape[0]):
            xt[tile] = solved[:, 128 * tile : 128 * (tile + 1)]

    half_update(part, True, parent, xt, coupling, sep, out, *scratch)


def keep_kernel(part, parent, xt, coupling, sep, out, *scratch):
    half_update(part, False, parent, xt, coupling, sep, out, *scratch)


def leaves(parent, rhs, inv, coupling, sep):
    n, width = coupling.shape[2], coupling.shape[3]
    leaf, cols = rhs.shape[2], rhs.shape[3]
    part, tiles = cols // 32, width // 128
    one = lambda *shape: pl.BlockSpec(shape, lambda k: (0,) * len(shape))
    per_level = [
        pl.BlockSpec((1, 1, 1, width, leaf), lambda k: (0, 0, k, 0, 0)),
        pl.BlockSpec((1, 1, 8, cols), lambda k: (0, k, 0, 0)),
    ]
    half_spec = pl.BlockSpec((2, 1, 1, tiles, 8 * part, 128), lambda k: (0, k // 2, k % 2, 0, 0, 0))
    half_shape = FLAT((2, 2, 2, tiles, 8 * part, 128), jnp.float32)
    xt_spec = one(leaf // 128, cols, 128)
    common = dict(
        grid=(n,),
        scratch_shapes=[
            pltpu.VMEM((cols // NC, leaf), jnp.bfloat16),
            pltpu.VMEM((cols // NC, leaf), jnp.bfloat16),
            pltpu.VMEM((128, cols), jnp.float32),
            pltpu.VMEM((1, cols, 128), jnp.float32),
        ],
        compiler_params=pltpu.CompilerParams(vmem_limit_bytes=24 * 2**20),
    )
    send, xt = pl.pallas_call(
        functools.partial(send_kernel, part),
        in_specs=[SMEM, one(1, 1, leaf, cols), one(1, 1, leaf, leaf)] + per_level,
        out_specs=[half_spec, xt_spec],
        out_shape=[half_shape, FLAT((leaf // 128, cols, 128), jnp.float32)],
        name="leaves_send",
        **common,
    )(parent, rhs, inv, coupling, sep)
    keep = pl.pallas_call(
        functools.partial(keep_kernel, part),
        in_specs=[SMEM, xt_spec] + per_level,
        out_specs=half_spec,
        out_shape=half_shape,
        name="leaves_keep",
        **common,
    )(parent, xt, coupling, sep)
    return send, keep


def sum_kernel(parts, out):
    count = out.shape[1]
    for s in range(8):
        rows = pl.ds(s, count, stride=8)
        out[s] = (parts[0, rows, :] + parts[1, rows, :]) + (parts[2, rows, :] + parts[3, rows, :])


def first_kernel(part, parts, weights, held, send, high, low, full, sems):
    x, _ = place()
    odd = x % 2 == 1

    def copies(m):
        return [
            pltpu.make_async_copy(
                weights.at[:, back, m],
                full.at[m, pl.ds(pl.multiple_of(((x + NX - back) % NX) * 16, 16), 16)],
                sems.at[m, back],
            )
            for back in range(NX)
        ]

    def matrix(m):
        for copy in copies(m):
            copy.wait()
        return split(full[m].reshape(-1, full.shape[3]))

    for m in range(4):
        for copy in copies(m):
            copy.start()

    @pl.when(odd)
    def _():
        for m in range(4, full.shape[0]):
            for copy in copies(m):
                copy.start()

    res = parts[0]
    for p in range(1, parts.shape[0]):
        res = res + parts[p]
    tiles = res.shape[0] // (2 * part)

    def residual(k):
        starts = [part * (tiles * k + tile) for tile in range(tiles)]
        return split(jnp.concatenate([res[at : at + part] for at in starts], axis=1))

    first = dot3(residual(0), matrix(0), NT)
    second = dot3(residual(1), matrix(1), NT)
    held[0] = first
    held[1] = second
    last = [matrix(2), matrix(3)]

    @pl.when(jnp.logical_not(odd))
    def _():
        chained = second - dot3(split(first), last[0], NT)
        shape = (part, held.shape[2])
        group = (lax.axis_index("c") * 2 + lax.axis_index("xl")) * NY + lax.axis_index("y")
        column = lax.broadcasted_iota(jnp.int32, shape, 0) + part * group
        mine = lax.broadcasted_iota(jnp.int32, shape, 1) == column
        pick = jnp.where(mine, jnp.where(lax.axis_index("layer") == 0, 1.0, 0.0), 0.0).astype(jnp.bfloat16)
        mm = functools.partial(lax.dot_general, dimension_numbers=NT, preferred_element_type=jnp.float32)
        held[1] = chained
        send[0] = chained
        send[1] = mm(pick, last[1][0]) + mm(pick, last[1][1])

    @pl.when(odd)
    def _():
        for at, pair in enumerate(last):
            high[at], low[at] = pair
        for m in range(4, full.shape[0]):
            high[m - 2], low[m - 2] = matrix(m)


def second_kernel(part, held, came, high, low, out, wide):
    wide[...] = jnp.zeros_like(wide)
    step = 40

    def store(at, value):
        for copy in range(3):
            wide[step * copy + part * at : step * copy + part * (at + 1), :] = value

    @pl.when(lax.axis_index("xh") == 0)
    def _():
        store(0, held[0])
        store(1, held[1])

    @pl.when(lax.axis_index("xh") == 1)
    def _():
        third = held[0] - dot3(split(came[0]), (high[0], low[0]), NT)
        store(0, third)
        fourth = held[1] - dot3(split(third), (high[1], low[1]), NT)
        store(1, fourth)
        term = came[1] - dot3(split(fourth), (high[2], low[2]), NT)
        store(2, dot3(split(term), (high[3], low[3]), NT))

    rows = wide[...].T.reshape(-1, 8, 128)
    lane = lax.broadcasted_iota(jnp.int32, (rows.shape[0], 1, 128), 2)
    for j in range(3):
        far = min(6 + j, 7)
        low_rows = jnp.where(lane < 80, rows[:, 3 + j : 4 + j], rows[:, far : far + 1])
        out[:, j : j + 1, :] = jnp.where(lane < 40, rows[:, j : j + 1], low_rows)


def unpack_kernel(part, got, sep, term, tall):
    for src in range(got.shape[0]):
        tall[8 * src : 8 * src + 3, :] = got[src]
        tall[8 * src + 3 : 8 * src + 6, :] = got[src]
        tall[8 * src + 6 : 8 * src + 8, :] = got[src, 0:2]
    flat = tall[...]
    row = lax.broadcasted_iota(jnp.int32, flat.shape, 0) % 8
    flat = jnp.where(
        row < 3, flat, jnp.where(row < 6, pltpu.roll(flat, 128 - 40, 1), pltpu.roll(flat, 128 - 80, 1))
    )
    lane = lax.broadcasted_iota(jnp.int32, (8, 128), 1)
    tiles = sep.shape[3] // 128
    full = [[jnp.zeros((8, 128), jnp.float32) for _ in range(tiles)] for _ in range(5)]
    for src in range(got.shape[0]):
        xl, xh, y, c = src // 32, src // 16 % 2, src // 2 % 8, src % 2
        block = flat[8 * src : 8 * src + 8]
        start = part * ((c * 2 + xl) * NY + y)
        for at in range(2 + xh):
            moved = pltpu.roll(block, (start - part * at) % 128, 1)
            to = 2 * xh + at
            for tile in range(start // 128, (start + part - 1) // 128 + 1):
                at_lane = lane + 128 * tile
                here = (at_lane >= start) & (at_lane < start + part)
                full[to][tile] = jnp.where(here, moved, full[to][tile])
    for tile in range(tiles):
        lanes = slice(128 * tile, 128 * (tile + 1))
        for k in range(4):
            sep[0, k, :, lanes] = full[k][tile]
        for layer in range(term.shape[0]):
            term[layer, :, lanes] = full[4][tile]


def in_hbm(array):
    return pltpu.with_memory_space_constraint(array, pltpu.HBM)


def body(
    leaf_rhs,
    leaf_inverse,
    leaf_coupling,
    parent,
    sep_rhs,
    sep_inverse,
    sep_coupling,
    root_coupling,
    root_rhs,
    root_inverse,
):
    width, cols = leaf_coupling.shape[3], leaf_rhs.shape[3]
    part = cols // 32
    tiles = width // 128
    call = pl.pallas_call

    same, other = call(
        pack_kernel,
        in_specs=[VMEM] * 5,
        out_specs=[VMEM, VMEM],
        out_shape=[FLAT((6, 8, width), jnp.float32)] * 2,
        name="pack",
    )(sep_inverse, sep_coupling, root_coupling, root_rhs, root_inverse)
    ring = [same] + [
        lax.ppermute(pack, X, [(i, (i + j) % NX) for i in range(NX)])
        for j, pack in ((1, other), (2, same), (3, other))
    ]

    weights = lax.all_gather(jnp.stack(ring), ("y", "c"))
    send, keep = leaves(parent, *map(in_hbm, (leaf_rhs, leaf_inverse, leaf_coupling, sep_rhs)))
    res = keep + lax.ppermute(send, "c", [(0, 1), (1, 0)])
    res = lax.all_to_all(res.reshape(NX, 2 * tiles * 8 * part, 128), X, 0, 0)
    res = call(
        sum_kernel,
        in_specs=[VMEM],
        out_specs=VMEM,
        out_shape=FLAT((8, 2 * tiles * part, 128), jnp.float32),
        compiler_params=pltpu.CompilerParams(vmem_limit_bytes=16 * 2**20),
        name="sum_x",
    )(res)
    res = lax.all_to_all(res, "y", 0, 0)

    held, send, high, low = call(
        functools.partial(first_kernel, part),
        in_specs=[VMEM, HBM],
        out_specs=[VMEM] * 4,
        out_shape=[FLAT((2, part, width), jnp.float32)] * 2 + [FLAT((4, width, width), jnp.bfloat16)] * 2,
        scratch_shapes=[pltpu.VMEM((6, 64, 8, width), jnp.float32), pltpu.SemaphoreType.DMA((6, NX))],
        compiler_params=pltpu.CompilerParams(vmem_limit_bytes=32 * 2**20),
        name="chain_first",
    )(res, in_hbm(weights))
    came = lax.ppermute(send, "xh", [(0, 1)])
    out = call(
        functools.partial(second_kernel, part),
        in_specs=[VMEM] * 4,
        out_specs=VMEM,
        out_shape=FLAT((64, 3, 128), jnp.float32),
        scratch_shapes=[pltpu.VMEM((128, width), jnp.float32)],
        compiler_params=pltpu.CompilerParams(vmem_limit_bytes=16 * 2**20),
        name="chain_second",
    )(held, came, high, low)

    out = lax.all_to_all(out, ROW, 0, 0)
    sep_out, term = call(
        functools.partial(unpack_kernel, part),
        in_specs=[VMEM],
        out_specs=[VMEM] * 2,
        out_shape=[FLAT((1, 4, 8, cols), jnp.float32), FLAT((8, 8, cols), jnp.float32)],
        scratch_shapes=[pltpu.VMEM((64 * 8, 128), jnp.float32)],
        name="unpack",
    )(out)
    root_out = lax.all_to_all(term, "layer", 0, 0).sum(0)
    return (sep_out, root_out)


def solution(mesh):
    fine = Mesh(mesh.devices.reshape(-1, 2, 2, NY, NC), ("layer",) + ROW)
    return jax.shard_map(
        body,
        mesh=fine,
        in_specs=(
            P("layer", ROW, None, None),
            P("layer", ROW, None, None),
            P("layer", ROW, None, None, None),
            P("layer", ROW),
            P("layer", None, ROW, None),
            P("layer", None, ROW, None),
            P("layer", None, ROW, None),
            P("layer", ROW, None),
            P(ROW, None),
            P(ROW, None),
        ),
        out_specs=(P("layer", None, ROW, None), P(ROW, None)),
        check_vma=False,
    )
```

```python
import functools

import jax
import jax.numpy as jnp
from jax import lax
from jax.experimental import pallas as pl
from jax.experimental.pallas import tpu as pltpu
from jax.sharding import Mesh, PartitionSpec as P

ROW = ("xl", "xh", "y", "c")
X = ("xl", "xh")
NX, NY, NC = 4, 8, 2
NT = (((1,), (1,)), ((), ()))
NN = (((1,), (0,)), ((), ()))
VMEM = pl.BlockSpec(memory_space=pltpu.VMEM)
SMEM = pl.BlockSpec(memory_space=pltpu.SMEM)
HBM = pl.BlockSpec(memory_space=pltpu.HBM)
FLAT = jax.ShapeDtypeStruct


def split(a):
    high = a.astype(jnp.bfloat16)
    return high, (a - high.astype(jnp.float32)).astype(jnp.bfloat16)


def dot3(a, b, dims):
    mm = functools.partial(lax.dot_general, dimension_numbers=dims, preferred_element_type=jnp.float32)
    return mm(a[0], b[0]) + (mm(a[0], b[1]) + mm(a[1], b[0]))


def by_tiles(ref, part):
    tiles, rows, _ = ref.shape

    def column(tile):
        return jnp.concatenate(
            [
                ref[tile, pl.ds(block + t, 8, stride=part), :]
                for block in range(0, rows, 8 * part)
                for t in range(part)
            ],
            axis=0,
        )

    return jnp.concatenate([column(tile) for tile in range(tiles)], axis=1)


def place():
    x = 2 * lax.axis_index("xl") + lax.axis_index("xh")
    return x, (x * NY + lax.axis_index("y")) * NC + lax.axis_index("c")


def pack_kernel(sep_inverse, sep_coupling, root_coupling, root_rhs, root_inverse, out):
    zeros = jnp.zeros_like(root_inverse)
    rr = jnp.concatenate([root_rhs[...], zeros[:, root_rhs.shape[1] :]], axis=1)
    tables = (
        [sep_inverse[0, 0], sep_inverse[0, 1], sep_coupling[0, 0], rr, zeros, zeros],
        [
            sep_inverse[0, 2],
            sep_inverse[0, 3],
            sep_coupling[0, 1],
            sep_coupling[0, 2],
            root_coupling[0],
            root_inverse[...],
        ],
    )
    for x in range(out.shape[0]):
        for m in range(out.shape[1]):
            out[x, m] = tables[x % 2][m]


def half_update(part, other, parent, xt, own, coupling, out, xt_hi, xt_lo):
    k = pl.program_id(0)
    core = lax.axis_index("c")
    count = xt.shape[0] // NC
    half = pl.ds(pl.multiple_of((1 - core if other else core) * count, 64), count)

    @pl.when(k == 0)
    def _():
        xt_hi[...], xt_lo[...] = split(xt[half, :])

    keep = jnp.where(k >= parent[0, 0], 1.0, 0.0)
    got = dot3((xt_hi[...], xt_lo[...]), split(coupling[0, 0, 0]), NT) * -keep
    block = place()[1]
    first = 8 * (block % 16)
    mine = pltpu.roll(own[half, :], (first - 8 * k + 128) % 128, 1)
    lane = lax.broadcasted_iota(jnp.int32, mine.shape, 1)
    mine = jnp.where((lane >= first) & (lane < first + 8), mine, 0.0)
    group = 8 * part
    for side in range(2):
        rows = slice(side * group, (side + 1) * group)
        for tile in range(out.shape[3]):
            out[side, 0, 0, tile] = got[rows, 128 * tile : 128 * (tile + 1)]
        out[side, 0, 0, block // 16] += mine[rows]


def send_kernel(part, parent, rhs, inv, sep, coupling, out, xt, own, plain, tall, flat, *scratch):
    @pl.when(pl.program_id(0) == 0)
    def _():
        solved = dot3(split(inv[0, 0]), split(rhs[0, 0]), NN).T
        for tile in range(plain.shape[0]):
            plain[tile] = solved[:, 128 * tile : 128 * (tile + 1)]
        xt[...] = by_tiles(plain, part)
        tall[...] = jnp.zeros_like(tall)
        for k in range(sep.shape[1]):
            tall[8 * k : 8 * k + 8, :] = sep[0, k]
        flat[0] = tall[...].T
        own[...] = by_tiles(flat, part)

    half_update(part, True, parent, xt, own, coupling, out, *scratch)


def keep_kernel(part, parent, xt, own, coupling, out, *scratch):
    half_update(part, False, parent, xt, own, coupling, out, *scratch)


def leaves(parent, rhs, inv, coupling, sep):
    n, width = coupling.shape[2], coupling.shape[3]
    leaf, cols = rhs.shape[2], rhs.shape[3]
    part, tiles = cols // 32, width // 128
    one = lambda *shape: pl.BlockSpec(shape, lambda k: (0,) * len(shape))
    coupling_spec = pl.BlockSpec((1, 1, 1, width, leaf), lambda k: (0, 0, k, 0, 0))
    half_spec = pl.BlockSpec((2, 1, 1, tiles, 8 * part, 128), lambda k: (0, k // 2, k % 2, 0, 0, 0))
    half_shape = FLAT((2, 2, 2, tiles, 8 * part, 128), jnp.float32)
    shared = [one(cols, leaf), one(cols, 128)]
    parts = [pltpu.VMEM((cols // NC, leaf), jnp.bfloat16)] * 2
    params = pltpu.CompilerParams(vmem_limit_bytes=24 * 2**20)
    send, xt, own = pl.pallas_call(
        functools.partial(send_kernel, part),
        grid=(n,),
        in_specs=[SMEM, one(1, 1, leaf, cols), one(1, 1, leaf, leaf), one(1, n, 8, cols), coupling_spec],
        out_specs=[half_spec] + shared,
        out_shape=[half_shape, FLAT((cols, leaf), jnp.float32), FLAT((cols, 128), jnp.float32)],
        scratch_shapes=[
            pltpu.VMEM((leaf // 128, cols, 128), jnp.float32),
            pltpu.VMEM((128, cols), jnp.float32),
            pltpu.VMEM((1, cols, 128), jnp.float32),
        ]
        + parts,
        compiler_params=params,
        name="leaves_send",
    )(parent, rhs, inv, sep, coupling)
    keep = pl.pallas_call(
        functools.partial(keep_kernel, part),
        grid=(n,),
        in_specs=[SMEM] + shared + [coupling_spec],
        out_specs=half_spec,
        out_shape=half_shape,
        scratch_shapes=parts,
        compiler_params=params,
        name="leaves_keep",
    )(parent, xt, own, coupling)
    return send, keep


def sum_kernel(parts, out):
    count = out.shape[1]
    for s in range(8):
        rows = pl.ds(s, count, stride=8)
        out[s] = (parts[0, rows, :] + parts[1, rows, :]) + (parts[2, rows, :] + parts[3, rows, :])


def first_kernel(part, parts, weights, held, send, high, low, full, sems):
    odd = lax.axis_index("xh") == 1

    def copies(m):
        return [
            pltpu.make_async_copy(
                weights.at[:, src, m], full.at[m, pl.ds(16 * src, 16)], sems.at[m, src]
            )
            for src in range(NX)
        ]

    def matrix(m):
        for copy in copies(m):
            copy.wait()
        return split(full[m].reshape(-1, full.shape[3]))

    for m in range(4):
        for copy in copies(m):
            copy.start()

    @pl.when(odd)
    def _():
        for m in range(4, full.shape[0]):
            for copy in copies(m):
                copy.start()

    res = parts[0]
    for p in range(1, parts.shape[0]):
        res = res + parts[p]
    tiles = res.shape[0] // (2 * part)

    def residual(k):
        starts = [part * (tiles * k + tile) for tile in range(tiles)]
        return split(jnp.concatenate([res[at : at + part] for at in starts], axis=1))

    first = dot3(residual(0), matrix(0), NT)
    second = dot3(residual(1), matrix(1), NT)
    held[0] = first
    held[1] = second
    last = [matrix(2), matrix(3)]

    @pl.when(jnp.logical_not(odd))
    def _():
        chained = second - dot3(split(first), last[0], NT)
        shape = (part, held.shape[2])
        group = (lax.axis_index("c") * 2 + lax.axis_index("xl")) * NY + lax.axis_index("y")
        column = lax.broadcasted_iota(jnp.int32, shape, 0) + part * group
        mine = lax.broadcasted_iota(jnp.int32, shape, 1) == column
        pick = jnp.where(mine, jnp.where(lax.axis_index("layer") == 0, 1.0, 0.0), 0.0).astype(jnp.bfloat16)
        mm = functools.partial(lax.dot_general, dimension_numbers=NT, preferred_element_type=jnp.float32)
        held[1] = chained
        send[0] = chained
        send[1] = mm(pick, last[1][0]) + mm(pick, last[1][1])

    @pl.when(odd)
    def _():
        for at, pair in enumerate(last):
            high[at], low[at] = pair
        for m in range(4, full.shape[0]):
            high[m - 2], low[m - 2] = matrix(m)


def second_kernel(part, held, came, high, low, out, wide):
    wide[...] = jnp.zeros_like(wide)
    step = 40

    def store(at, value):
        for copy in range(3):
            wide[step * copy + part * at : step * copy + part * (at + 1), :] = value

    @pl.when(lax.axis_index("xh") == 0)
    def _():
        store(0, held[0])
        store(1, held[1])

    @pl.when(lax.axis_index("xh") == 1)
    def _():
        third = held[0] - dot3(split(came[0]), (high[0], low[0]), NT)
        store(0, third)
        fourth = held[1] - dot3(split(third), (high[1], low[1]), NT)
        store(1, fourth)
        term = came[1] - dot3(split(fourth), (high[2], low[2]), NT)
        store(2, dot3(split(term), (high[3], low[3]), NT))

    rows = wide[...].T.reshape(-1, 8, 128)
    lane = lax.broadcasted_iota(jnp.int32, (rows.shape[0], 1, 128), 2)
    for j in range(3):
        far = min(6 + j, 7)
        low_rows = jnp.where(lane < 80, rows[:, 3 + j : 4 + j], rows[:, far : far + 1])
        out[:, j : j + 1, :] = jnp.where(lane < 40, rows[:, j : j + 1], low_rows)


def unpack_kernel(part, got, sep, term, tall):
    for src in range(got.shape[0]):
        tall[8 * src : 8 * src + 3, :] = got[src]
        tall[8 * src + 3 : 8 * src + 6, :] = got[src]
        tall[8 * src + 6 : 8 * src + 8, :] = got[src, 0:2]
    flat = tall[...]
    row = lax.broadcasted_iota(jnp.int32, flat.shape, 0) % 8
    flat = jnp.where(
        row < 3, flat, jnp.where(row < 6, pltpu.roll(flat, 128 - 40, 1), pltpu.roll(flat, 128 - 80, 1))
    )
    lane = lax.broadcasted_iota(jnp.int32, (8, 128), 1)
    tiles = sep.shape[3] // 128
    full = [[jnp.zeros((8, 128), jnp.float32) for _ in range(tiles)] for _ in range(5)]
    for src in range(got.shape[0]):
        xl, xh, y, c = src // 32, src // 16 % 2, src // 2 % 8, src % 2
        block = flat[8 * src : 8 * src + 8]
        start = part * ((c * 2 + xl) * NY + y)
        for at in range(2 + xh):
            moved = pltpu.roll(block, (start - part * at) % 128, 1)
            to = 2 * xh + at
            for tile in range(start // 128, (start + part - 1) // 128 + 1):
                at_lane = lane + 128 * tile
                here = (at_lane >= start) & (at_lane < start + part)
                full[to][tile] = jnp.where(here, moved, full[to][tile])
    for tile in range(tiles):
        lanes = slice(128 * tile, 128 * (tile + 1))
        for k in range(4):
            sep[0, k, :, lanes] = full[k][tile]
        for layer in range(term.shape[0]):
            term[layer, :, lanes] = full[4][tile]


def in_hbm(array):
    return pltpu.with_memory_space_constraint(array, pltpu.HBM)


def in_vmem(array):
    return pltpu.with_memory_space_constraint(array, pltpu.VMEM)


def body(
    leaf_rhs,
    leaf_inverse,
    leaf_coupling,
    parent,
    sep_rhs,
    sep_inverse,
    sep_coupling,
    root_coupling,
    root_rhs,
    root_inverse,
):
    width, cols = leaf_coupling.shape[3], leaf_rhs.shape[3]
    part = cols // 32
    tiles = width // 128
    call = pl.pallas_call

    pack = call(
        pack_kernel,
        in_specs=[VMEM] * 5,
        out_specs=VMEM,
        out_shape=FLAT((NX, 6, 8, width), jnp.float32),
        name="pack",
    )(sep_inverse, sep_coupling, root_coupling, root_rhs, root_inverse)
    weights = lax.all_gather(lax.all_to_all(pack, X, 0, 0), ("y", "c"))
    send, keep = leaves(parent, *map(in_hbm, (leaf_rhs, leaf_inverse, leaf_coupling, sep_rhs)))
    res = keep + lax.ppermute(send, "c", [(0, 1), (1, 0)])
    res = lax.all_to_all(res.reshape(NX, 2 * tiles * 8 * part, 128), X, 0, 0)
    res = call(
        sum_kernel,
        in_specs=[VMEM],
        out_specs=VMEM,
        out_shape=FLAT((8, 2 * tiles * part, 128), jnp.float32),
        compiler_params=pltpu.CompilerParams(vmem_limit_bytes=16 * 2**20),
        name="sum_x",
    )(res)
    res = lax.all_to_all(res, "y", 0, 0)

    held, send, high, low = call(
        functools.partial(first_kernel, part),
        in_specs=[VMEM, HBM],
        out_specs=[VMEM] * 4,
        out_shape=[FLAT((2, part, width), jnp.float32)] * 2 + [FLAT((4, width, width), jnp.bfloat16)] * 2,
        scratch_shapes=[pltpu.VMEM((6, 64, 8, width), jnp.float32), pltpu.SemaphoreType.DMA((6, NX))],
        compiler_params=pltpu.CompilerParams(vmem_limit_bytes=32 * 2**20),
        name="chain_first",
    )(res, in_hbm(weights))
    came = lax.ppermute(send, "xh", [(0, 1)])
    out = call(
        functools.partial(second_kernel, part),
        in_specs=[VMEM] * 4,
        out_specs=VMEM,
        out_shape=pltpu.VMEM((64, 3, 128), jnp.float32),
        scratch_shapes=[pltpu.VMEM((128, width), jnp.float32)],
        compiler_params=pltpu.CompilerParams(vmem_limit_bytes=16 * 2**20),
        name="chain_second",
    )(held, came, high, low)

    out = lax.all_to_all(out, ROW, 0, 0)
    sep_out, term = call(
        functools.partial(unpack_kernel, part),
        in_specs=[VMEM],
        out_specs=[VMEM] * 2,
        out_shape=[FLAT((1, 4, 8, cols), jnp.float32), pltpu.VMEM((8, 8, cols), jnp.float32)],
        scratch_shapes=[pltpu.VMEM((64 * 8, 128), jnp.float32)],
        name="unpack",
    )(in_vmem(out))
    root_out = lax.all_to_all(term, "layer", 0, 0).sum(0)
    return (sep_out, root_out)


def solution(mesh):
    fine = Mesh(mesh.devices.reshape(-1, 2, 2, NY, NC), ("layer",) + ROW)
    return jax.shard_map(
        body,
        mesh=fine,
        in_specs=(
            P("layer", ROW, None, None),
            P("layer", ROW, None, None),
            P("layer", ROW, None, None, None),
            P("layer", ROW),
            P("layer", None, ROW, None),
            P("layer", None, ROW, None),
            P("layer", None, ROW, None),
            P("layer", ROW, None),
            P(ROW, None),
            P(ROW, None),
        ),
        out_specs=(P("layer", None, ROW, None), P(ROW, None)),
        check_vma=False,
    )
```

```python
import functools

import jax
import jax.numpy as jnp
from jax import lax
from jax.experimental import pallas as pl
from jax.experimental.pallas import tpu as pltpu
from jax.sharding import Mesh, PartitionSpec as P

ROW = ("xl", "xh", "y", "c")
X = ("xl", "xh")
NX, NY, NC = 4, 8, 2
NT = (((1,), (1,)), ((), ()))
NN = (((1,), (0,)), ((), ()))
VMEM = pl.BlockSpec(memory_space=pltpu.VMEM)
SMEM = pl.BlockSpec(memory_space=pltpu.SMEM)
HBM = pl.BlockSpec(memory_space=pltpu.HBM)
FLAT = jax.ShapeDtypeStruct


def split(a):
    high = a.astype(jnp.bfloat16)
    return high, (a - high.astype(jnp.float32)).astype(jnp.bfloat16)


def stack(a):
    return jnp.concatenate(split(a), axis=0)


def dot3(a, b, dims):
    mm = functools.partial(lax.dot_general, dimension_numbers=dims, preferred_element_type=jnp.float32)
    rows = a.shape[0] // 2
    both = mm(a, b[0])
    return both[:rows] + (both[rows:] + mm(a[:rows], b[1]))


def by_tiles(ref, part):
    tiles, rows, _ = ref.shape

    def column(tile):
        return jnp.concatenate(
            [
                ref[tile, pl.ds(block + t, 8, stride=part), :]
                for block in range(0, rows, 8 * part)
                for t in range(part)
            ],
            axis=0,
        )

    return jnp.concatenate([column(tile) for tile in range(tiles)], axis=1)


def place():
    x = 2 * lax.axis_index("xl") + lax.axis_index("xh")
    return x, (x * NY + lax.axis_index("y")) * NC + lax.axis_index("c")


def pack_kernel(sep_inverse, sep_coupling, root_coupling, root_rhs, root_inverse, out):
    zeros = jnp.zeros_like(root_inverse)
    rr = jnp.concatenate([root_rhs[...], zeros[:, root_rhs.shape[1] :]], axis=1)
    tables = (
        [sep_inverse[0, 0], sep_inverse[0, 1], sep_coupling[0, 0], rr, zeros, zeros],
        [
            sep_inverse[0, 2],
            sep_inverse[0, 3],
            sep_coupling[0, 1],
            sep_coupling[0, 2],
            root_coupling[0],
            root_inverse[...],
        ],
    )
    for x in range(out.shape[0]):
        for m in range(out.shape[1]):
            out[x, m] = tables[x % 2][m]


def half_update(part, other, parent, xt, own, coupling, out, pair):
    k = pl.program_id(0)
    core = lax.axis_index("c")
    count = xt.shape[0] // NC
    half = pl.ds(pl.multiple_of((1 - core if other else core) * count, 64), count)

    @pl.when(k == 0)
    def _():
        pair[...] = stack(xt[half, :])

    keep = jnp.where(k >= parent[0, 0], 1.0, 0.0)
    got = dot3(pair[...], split(coupling[0, 0, 0]), NT) * -keep
    block = place()[1]
    first = 8 * (block % 16)
    mine = pltpu.roll(own[half, :], (first - 8 * k + 128) % 128, 1)
    lane = lax.broadcasted_iota(jnp.int32, mine.shape, 1)
    mine = jnp.where((lane >= first) & (lane < first + 8), mine, 0.0)
    group = 8 * part
    for side in range(2):
        rows = slice(side * group, (side + 1) * group)
        for tile in range(out.shape[3]):
            out[side, 0, 0, tile] = got[rows, 128 * tile : 128 * (tile + 1)]
        out[side, 0, 0, block // 16] += mine[rows]


def send_kernel(part, parent, rhs, inv, sep, coupling, out, xt, own, plain, tall, flat, *scratch):
    @pl.when(pl.program_id(0) == 0)
    def _():
        solved = dot3(stack(inv[0, 0]), split(rhs[0, 0]), NN).T
        for tile in range(plain.shape[0]):
            plain[tile] = solved[:, 128 * tile : 128 * (tile + 1)]
        xt[...] = by_tiles(plain, part)
        tall[...] = jnp.zeros_like(tall)
        for k in range(sep.shape[1]):
            tall[8 * k : 8 * k + 8, :] = sep[0, k]
        flat[0] = tall[...].T
        own[...] = by_tiles(flat, part)

    half_update(part, True, parent, xt, own, coupling, out, *scratch)


def keep_kernel(part, parent, xt, own, coupling, out, *scratch):
    half_update(part, False, parent, xt, own, coupling, out, *scratch)


def leaf_specs(coupling, cols):
    n, width, leaf = coupling.shape[2:]
    part, tiles = cols // 32, width // 128
    one = lambda *shape: pl.BlockSpec(shape, lambda k: (0,) * len(shape))
    coupling_spec = pl.BlockSpec((1, 1, 1, width, leaf), lambda k: (0, 0, k, 0, 0))
    half_spec = pl.BlockSpec((2, 1, 1, tiles, 8 * part, 128), lambda k: (0, k // 2, k % 2, 0, 0, 0))
    half_shape = FLAT((2, 2, 2, tiles, 8 * part, 128), jnp.float32)
    shared = [one(cols, leaf), one(cols, 128)]
    pair = pltpu.VMEM((2 * (cols // NC), leaf), jnp.bfloat16)
    params = pltpu.CompilerParams(vmem_limit_bytes=24 * 2**20)
    return part, one, coupling_spec, half_spec, half_shape, shared, pair, params


def leaves_send(parent, rhs, inv, coupling, sep):
    n, leaf, cols = coupling.shape[2], rhs.shape[2], rhs.shape[3]
    part, one, coupling_spec, half_spec, half_shape, shared, pair, params = leaf_specs(coupling, cols)
    return pl.pallas_call(
        functools.partial(send_kernel, part),
        grid=(n,),
        in_specs=[SMEM, one(1, 1, leaf, cols), one(1, 1, leaf, leaf), one(1, n, 8, cols), coupling_spec],
        out_specs=[half_spec] + shared,
        out_shape=[half_shape, FLAT((cols, leaf), jnp.float32), FLAT((cols, 128), jnp.float32)],
        scratch_shapes=[
            pltpu.VMEM((leaf // 128, cols, 128), jnp.float32),
            pltpu.VMEM((128, cols), jnp.float32),
            pltpu.VMEM((1, cols, 128), jnp.float32),
            pair,
        ],
        compiler_params=params,
        name="leaves_send",
    )(parent, rhs, inv, sep, coupling)


def leaves_keep(parent, xt, own, coupling):
    part, _, coupling_spec, half_spec, half_shape, shared, pair, params = leaf_specs(coupling, xt.shape[0])
    return pl.pallas_call(
        functools.partial(keep_kernel, part),
        grid=(coupling.shape[2],),
        in_specs=[SMEM] + shared + [coupling_spec],
        out_specs=half_spec,
        out_shape=half_shape,
        scratch_shapes=[pair],
        compiler_params=params,
        name="leaves_keep",
    )(parent, xt, own, coupling)


def sum_kernel(parts, out):
    count = out.shape[1]
    for s in range(8):
        rows = pl.ds(s, count, stride=8)
        out[s] = (parts[0, rows, :] + parts[1, rows, :]) + (parts[2, rows, :] + parts[3, rows, :])


def first_kernel(part, parts, weights, held, send, high, low, full, sems):
    odd = lax.axis_index("xh") == 1

    def copies(m):
        return [
            pltpu.make_async_copy(
                weights.at[:, src, m], full.at[m, pl.ds(16 * src, 16)], sems.at[m, src]
            )
            for src in range(NX)
        ]

    def matrix(m):
        for copy in copies(m):
            copy.wait()
        return split(full[m].reshape(-1, full.shape[3]))

    for m in range(4):
        for copy in copies(m):
            copy.start()

    @pl.when(odd)
    def _():
        for m in range(4, full.shape[0]):
            for copy in copies(m):
                copy.start()

    res = parts[0]
    for p in range(1, parts.shape[0]):
        res = res + parts[p]
    tiles = res.shape[0] // (2 * part)

    def residual(k):
        starts = [part * (tiles * k + tile) for tile in range(tiles)]
        rows = jnp.concatenate([res[at : at + part] for at in starts], axis=1)
        return stack(jnp.concatenate([rows, jnp.zeros((16 - part, rows.shape[1]), jnp.float32)], axis=0))

    first = dot3(residual(0), matrix(0), NT)
    second = dot3(residual(1), matrix(1), NT)
    held[0] = first
    held[1] = second
    last = [matrix(2), matrix(3)]

    @pl.when(jnp.logical_not(odd))
    def _():
        chained = second - dot3(stack(first), last[0], NT)
        shape = held.shape[1:]
        group = (lax.axis_index("c") * 2 + lax.axis_index("xl")) * NY + lax.axis_index("y")
        column = lax.broadcasted_iota(jnp.int32, shape, 0) + part * group
        mine = lax.broadcasted_iota(jnp.int32, shape, 1) == column
        pick = jnp.where(mine, jnp.where(lax.axis_index("layer") == 0, 1.0, 0.0), 0.0).astype(jnp.bfloat16)
        mm = functools.partial(lax.dot_general, dimension_numbers=NT, preferred_element_type=jnp.float32)
        held[1] = chained
        send[0] = chained
        send[1] = mm(pick, last[1][0]) + mm(pick, last[1][1])

    @pl.when(odd)
    def _():
        for at, pair in enumerate(last):
            high[at], low[at] = pair
        for m in range(4, full.shape[0]):
            high[m - 2], low[m - 2] = matrix(m)


def second_kernel(part, held, came, high, low, out, wide):
    wide[...] = jnp.zeros_like(wide)
    step = 40

    def store(at, value):
        for copy in range(3):
            wide[step * copy + part * at : step * copy + part * (at + 1), :] = value[:part]

    @pl.when(lax.axis_index("xh") == 0)
    def _():
        store(0, held[0])
        store(1, held[1])

    @pl.when(lax.axis_index("xh") == 1)
    def _():
        third = held[0] - dot3(stack(came[0]), (high[0], low[0]), NT)
        store(0, third)
        fourth = held[1] - dot3(stack(third), (high[1], low[1]), NT)
        store(1, fourth)
        term = came[1] - dot3(stack(fourth), (high[2], low[2]), NT)
        store(2, dot3(stack(term), (high[3], low[3]), NT))

    rows = wide[...].T.reshape(-1, 8, 128)
    lane = lax.broadcasted_iota(jnp.int32, (rows.shape[0], 1, 128), 2)
    for j in range(3):
        far = min(6 + j, 7)
        low_rows = jnp.where(lane < 80, rows[:, 3 + j : 4 + j], rows[:, far : far + 1])
        out[:, j : j + 1, :] = jnp.where(lane < 40, rows[:, j : j + 1], low_rows)


def unpack_kernel(part, got, sep, term, tall):
    for src in range(got.shape[0]):
        tall[8 * src : 8 * src + 3, :] = got[src]
        tall[8 * src + 3 : 8 * src + 6, :] = got[src]
        tall[8 * src + 6 : 8 * src + 8, :] = got[src, 0:2]
    flat = tall[...]
    row = lax.broadcasted_iota(jnp.int32, flat.shape, 0) % 8
    flat = jnp.where(
        row < 3, flat, jnp.where(row < 6, pltpu.roll(flat, 128 - 40, 1), pltpu.roll(flat, 128 - 80, 1))
    )
    lane = lax.broadcasted_iota(jnp.int32, (8, 128), 1)
    tiles = sep.shape[3] // 128
    full = [[jnp.zeros((8, 128), jnp.float32) for _ in range(tiles)] for _ in range(5)]
    for src in range(got.shape[0]):
        xl, xh, y, c = src // 32, src // 16 % 2, src // 2 % 8, src % 2
        block = flat[8 * src : 8 * src + 8]
        start = part * ((c * 2 + xl) * NY + y)
        for at in range(2 + xh):
            moved = pltpu.roll(block, (start - part * at) % 128, 1)
            to = 2 * xh + at
            for tile in range(start // 128, (start + part - 1) // 128 + 1):
                at_lane = lane + 128 * tile
                here = (at_lane >= start) & (at_lane < start + part)
                full[to][tile] = jnp.where(here, moved, full[to][tile])
    for tile in range(tiles):
        lanes = slice(128 * tile, 128 * (tile + 1))
        for k in range(4):
            sep[0, k, :, lanes] = full[k][tile]
        for layer in range(term.shape[0]):
            term[layer, :, lanes] = full[4][tile]


def in_hbm(array):
    return pltpu.with_memory_space_constraint(array, pltpu.HBM)


def in_vmem(array):
    return pltpu.with_memory_space_constraint(array, pltpu.VMEM)


def body(
    leaf_rhs,
    leaf_inverse,
    leaf_coupling,
    parent,
    sep_rhs,
    sep_inverse,
    sep_coupling,
    root_coupling,
    root_rhs,
    root_inverse,
):
    width, cols = leaf_coupling.shape[3], leaf_rhs.shape[3]
    part = cols // 32
    tiles = width // 128
    call = pl.pallas_call

    pack = call(
        pack_kernel,
        in_specs=[VMEM] * 5,
        out_specs=VMEM,
        out_shape=FLAT((NX, 6, 8, width), jnp.float32),
        name="pack",
    )(sep_inverse, sep_coupling, root_coupling, root_rhs, root_inverse)
    exchanged = lax.all_to_all(pack, X, 0, 0)

    leaf_rhs, leaf_inverse, leaf_coupling, sep_rhs = map(
        in_hbm, (leaf_rhs, leaf_inverse, leaf_coupling, sep_rhs)
    )
    send, xt, own = leaves_send(parent, leaf_rhs, leaf_inverse, leaf_coupling, sep_rhs)
    exchanged, xt = lax.optimization_barrier((exchanged, xt))
    weights = lax.all_gather(exchanged, ("y", "c"))
    keep = leaves_keep(parent, xt, own, leaf_coupling)
    res = keep + lax.ppermute(send, "c", [(0, 1), (1, 0)])
    res = lax.all_to_all(res.reshape(NX, 2 * tiles * 8 * part, 128), X, 0, 0)
    res = call(
        sum_kernel,
        in_specs=[VMEM],
        out_specs=VMEM,
        out_shape=FLAT((8, 2 * tiles * part, 128), jnp.float32),
        compiler_params=pltpu.CompilerParams(vmem_limit_bytes=16 * 2**20),
        name="sum_x",
    )(res)
    res = lax.all_to_all(res, "y", 0, 0)

    held, send, high, low = call(
        functools.partial(first_kernel, part),
        in_specs=[VMEM, HBM],
        out_specs=[VMEM] * 4,
        out_shape=[FLAT((2, 16, width), jnp.float32)] * 2 + [FLAT((4, width, width), jnp.bfloat16)] * 2,
        scratch_shapes=[pltpu.VMEM((6, 64, 8, width), jnp.float32), pltpu.SemaphoreType.DMA((6, NX))],
        compiler_params=pltpu.CompilerParams(vmem_limit_bytes=32 * 2**20),
        name="chain_first",
    )(res, in_hbm(weights))
    came = lax.ppermute(send, "xh", [(0, 1)])
    out = call(
        functools.partial(second_kernel, part),
        in_specs=[VMEM] * 4,
        out_specs=VMEM,
        out_shape=pltpu.VMEM((64, 3, 128), jnp.float32),
        scratch_shapes=[pltpu.VMEM((128, width), jnp.float32)],
        compiler_params=pltpu.CompilerParams(vmem_limit_bytes=16 * 2**20),
        name="chain_second",
    )(held, came, high, low)

    out = lax.all_to_all(out, ROW, 0, 0)
    sep_out, term = call(
        functools.partial(unpack_kernel, part),
        in_specs=[VMEM],
        out_specs=[VMEM] * 2,
        out_shape=[FLAT((1, 4, 8, cols), jnp.float32), pltpu.VMEM((8, 8, cols), jnp.float32)],
        scratch_shapes=[pltpu.VMEM((64 * 8, 128), jnp.float32)],
        name="unpack",
    )(in_vmem(out))
    root_out = lax.all_to_all(term, "layer", 0, 0).sum(0)
    return (sep_out, root_out)


def solution(mesh):
    fine = Mesh(mesh.devices.reshape(-1, 2, 2, NY, NC), ("layer",) + ROW)
    return jax.shard_map(
        body,
        mesh=fine,
        in_specs=(
            P("layer", ROW, None, None),
            P("layer", ROW, None, None),
            P("layer", ROW, None, None, None),
            P("layer", ROW),
            P("layer", None, ROW, None),
            P("layer", None, ROW, None),
            P("layer", None, ROW, None),
            P("layer", ROW, None),
            P(ROW, None),
            P(ROW, None),
        ),
        out_specs=(P("layer", None, ROW, None), P(ROW, None)),
        check_vma=False,
    )
```

```python
import functools

import jax
import jax.numpy as jnp
from jax import lax
from jax.experimental import pallas as pl
from jax.experimental.pallas import tpu as pltpu
from jax.sharding import Mesh, PartitionSpec as P

ROW = ("xl", "xh", "y", "c")
X = ("xl", "xh")
NX, NY, NC = 4, 8, 2
NT = (((1,), (1,)), ((), ()))
NN = (((1,), (0,)), ((), ()))
VMEM = pl.BlockSpec(memory_space=pltpu.VMEM)
SMEM = pl.BlockSpec(memory_space=pltpu.SMEM)
HBM = pl.BlockSpec(memory_space=pltpu.HBM)
FLAT = jax.ShapeDtypeStruct


def split(a):
    high = a.astype(jnp.bfloat16)
    return high, (a - high.astype(jnp.float32)).astype(jnp.bfloat16)


def stack(a):
    return jnp.concatenate(split(a), axis=0)


def dot3(a, b, dims):
    mm = functools.partial(lax.dot_general, dimension_numbers=dims, preferred_element_type=jnp.float32)
    rows = a.shape[0] // 2
    both = mm(a, b[0])
    return both[:rows] + (both[rows:] + mm(a[:rows], b[1]))


def by_tiles(ref, part):
    tiles, rows, _ = ref.shape

    def column(tile):
        return jnp.concatenate(
            [
                ref[tile, pl.ds(block + t, 8, stride=part), :]
                for block in range(0, rows, 8 * part)
                for t in range(part)
            ],
            axis=0,
        )

    return jnp.concatenate([column(tile) for tile in range(tiles)], axis=1)


def place():
    x = 2 * lax.axis_index("xl") + lax.axis_index("xh")
    return x, (x * NY + lax.axis_index("y")) * NC + lax.axis_index("c")


def pack_kernel(sep_inverse, sep_coupling, root_coupling, root_rhs, root_inverse, out):
    zeros = jnp.zeros_like(root_inverse)
    rr = jnp.concatenate([root_rhs[...], zeros[:, root_rhs.shape[1] :]], axis=1)
    tables = (
        [sep_inverse[0, 0], sep_inverse[0, 1], sep_coupling[0, 0], sep_coupling[0, 1], rr],
        [sep_inverse[0, 2], sep_inverse[0, 3], sep_coupling[0, 2], root_coupling[0], root_inverse[...]],
    )
    for x in range(out.shape[0]):
        for m in range(out.shape[1]):
            out[x, m] = tables[x % 2][m]


def half_update(part, other, parent, xt, own, coupling, out, pair):
    k = pl.program_id(0)
    core = lax.axis_index("c")
    count = xt.shape[0] // NC
    half = pl.ds(pl.multiple_of((1 - core if other else core) * count, 64), count)

    @pl.when(k == 0)
    def _():
        pair[...] = stack(xt[half, :])

    keep = jnp.where(k >= parent[0, 0], 1.0, 0.0)
    got = dot3(pair[...], split(coupling[0, 0, 0]), NT) * -keep
    block = place()[1]
    first = 8 * (block % 16)
    mine = pltpu.roll(own[half, :], (first - 8 * k + 128) % 128, 1)
    lane = lax.broadcasted_iota(jnp.int32, mine.shape, 1)
    mine = jnp.where((lane >= first) & (lane < first + 8), mine, 0.0)
    group = 8 * part
    for side in range(2):
        rows = slice(side * group, (side + 1) * group)
        for tile in range(out.shape[3]):
            out[side, 0, 0, tile] = got[rows, 128 * tile : 128 * (tile + 1)]
        out[side, 0, 0, block // 16] += mine[rows]


def send_kernel(part, parent, rhs, inv, sep, coupling, out, xt, own, plain, tall, flat, *scratch):
    @pl.when(pl.program_id(0) == 0)
    def _():
        solved = dot3(stack(inv[0, 0]), split(rhs[0, 0]), NN).T
        for tile in range(plain.shape[0]):
            plain[tile] = solved[:, 128 * tile : 128 * (tile + 1)]
        xt[...] = by_tiles(plain, part)
        tall[...] = jnp.zeros_like(tall)
        for k in range(sep.shape[1]):
            tall[8 * k : 8 * k + 8, :] = sep[0, k]
        flat[0] = tall[...].T
        own[...] = by_tiles(flat, part)

    half_update(part, True, parent, xt, own, coupling, out, *scratch)


def keep_kernel(part, parent, xt, own, coupling, out, *scratch):
    half_update(part, False, parent, xt, own, coupling, out, *scratch)


def leaf_specs(coupling, cols):
    n, width, leaf = coupling.shape[2:]
    part, tiles = cols // 32, width // 128
    one = lambda *shape: pl.BlockSpec(shape, lambda k: (0,) * len(shape))
    coupling_spec = pl.BlockSpec((1, 1, 1, width, leaf), lambda k: (0, 0, k, 0, 0))
    half_spec = pl.BlockSpec((2, 1, 1, tiles, 8 * part, 128), lambda k: (0, k // 2, k % 2, 0, 0, 0))
    half_shape = FLAT((2, 2, 2, tiles, 8 * part, 128), jnp.float32)
    shared = [one(cols, leaf), one(cols, 128)]
    pair = pltpu.VMEM((2 * (cols // NC), leaf), jnp.bfloat16)
    params = pltpu.CompilerParams(vmem_limit_bytes=24 * 2**20)
    return part, one, coupling_spec, half_spec, half_shape, shared, pair, params


def leaves_send(parent, rhs, inv, coupling, sep):
    n, leaf, cols = coupling.shape[2], rhs.shape[2], rhs.shape[3]
    part, one, coupling_spec, half_spec, half_shape, shared, pair, params = leaf_specs(coupling, cols)
    return pl.pallas_call(
        functools.partial(send_kernel, part),
        grid=(n,),
        in_specs=[SMEM, one(1, 1, leaf, cols), one(1, 1, leaf, leaf), one(1, n, 8, cols), coupling_spec],
        out_specs=[half_spec] + shared,
        out_shape=[half_shape, FLAT((cols, leaf), jnp.float32), FLAT((cols, 128), jnp.float32)],
        scratch_shapes=[
            pltpu.VMEM((leaf // 128, cols, 128), jnp.float32),
            pltpu.VMEM((128, cols), jnp.float32),
            pltpu.VMEM((1, cols, 128), jnp.float32),
            pair,
        ],
        compiler_params=params,
        name="leaves_send",
    )(parent, rhs, inv, sep, coupling)


def leaves_keep(parent, xt, own, coupling):
    part, _, coupling_spec, half_spec, half_shape, shared, pair, params = leaf_specs(coupling, xt.shape[0])
    return pl.pallas_call(
        functools.partial(keep_kernel, part),
        grid=(coupling.shape[2],),
        in_specs=[SMEM] + shared + [coupling_spec],
        out_specs=half_spec,
        out_shape=half_shape,
        scratch_shapes=[pair],
        compiler_params=params,
        name="leaves_keep",
    )(parent, xt, own, coupling)


def sum_kernel(parts, out):
    count = out.shape[1]
    for s in range(8):
        rows = pl.ds(s, count, stride=8)
        out[s] = (parts[0, rows, :] + parts[1, rows, :]) + (parts[2, rows, :] + parts[3, rows, :])


def first_kernel(part, parts, weights, held, send, high, low, full, sems):
    odd = lax.axis_index("xh") == 1

    def copies(m):
        return [
            pltpu.make_async_copy(
                weights.at[:, src, m], full.at[m, pl.ds(16 * src, 16)], sems.at[m, src]
            )
            for src in range(NX)
        ]

    def matrix(m):
        for copy in copies(m):
            copy.wait()
        return split(full[m].reshape(-1, full.shape[3]))

    for m in range(full.shape[0]):
        for copy in copies(m):
            copy.start()

    res = parts[0]
    for p in range(1, parts.shape[0]):
        res = res + parts[p]
    tiles = res.shape[0] // (2 * part)

    def residual(k):
        starts = [part * (tiles * k + tile) for tile in range(tiles)]
        rows = jnp.concatenate([res[at : at + part] for at in starts], axis=1)
        return stack(jnp.concatenate([rows, jnp.zeros((16 - part, rows.shape[1]), jnp.float32)], axis=0))

    first = dot3(residual(0), matrix(0), NT)
    second = dot3(residual(1), matrix(1), NT)
    held[0] = first
    held[1] = second

    @pl.when(jnp.logical_not(odd))
    def _():
        chained = second - dot3(stack(first), matrix(2), NT)
        held[1] = chained
        send[0] = dot3(stack(chained), matrix(3), NT)
        shape = held.shape[1:]
        group = (lax.axis_index("c") * 2 + lax.axis_index("xl")) * NY + lax.axis_index("y")
        column = lax.broadcasted_iota(jnp.int32, shape, 0) + part * group
        mine = lax.broadcasted_iota(jnp.int32, shape, 1) == column
        pick = jnp.where(mine, jnp.where(lax.axis_index("layer") == 0, 1.0, 0.0), 0.0).astype(jnp.bfloat16)
        mm = functools.partial(lax.dot_general, dimension_numbers=NT, preferred_element_type=jnp.float32)
        rhs_high, rhs_low = matrix(4)
        send[1] = mm(pick, rhs_high) + mm(pick, rhs_low)

    @pl.when(odd)
    def _():
        for m in range(2, full.shape[0]):
            high[m - 2], low[m - 2] = matrix(m)


def second_kernel(part, held, came, high, low, out, wide):
    wide[...] = jnp.zeros_like(wide)
    step = 40

    def store(at, value):
        for copy in range(3):
            wide[step * copy + part * at : step * copy + part * (at + 1), :] = value[:part]

    @pl.when(lax.axis_index("xh") == 0)
    def _():
        store(0, held[0])
        store(1, held[1])

    @pl.when(lax.axis_index("xh") == 1)
    def _():
        third = held[0] - came[0]
        store(0, third)
        fourth = held[1] - dot3(stack(third), (high[0], low[0]), NT)
        store(1, fourth)
        term = came[1] - dot3(stack(fourth), (high[1], low[1]), NT)
        store(2, dot3(stack(term), (high[2], low[2]), NT))

    rows = wide[...].T.reshape(-1, 8, 128)
    lane = lax.broadcasted_iota(jnp.int32, (rows.shape[0], 1, 128), 2)
    for j in range(3):
        far = min(6 + j, 7)
        low_rows = jnp.where(lane < 80, rows[:, 3 + j : 4 + j], rows[:, far : far + 1])
        out[:, j : j + 1, :] = jnp.where(lane < 40, rows[:, j : j + 1], low_rows)


def unpack_kernel(part, got, sep, term, tall):
    for src in range(got.shape[0]):
        tall[8 * src : 8 * src + 3, :] = got[src]
        tall[8 * src + 3 : 8 * src + 6, :] = got[src]
        tall[8 * src + 6 : 8 * src + 8, :] = got[src, 0:2]
    flat = tall[...]
    row = lax.broadcasted_iota(jnp.int32, flat.shape, 0) % 8
    flat = jnp.where(
        row < 3, flat, jnp.where(row < 6, pltpu.roll(flat, 128 - 40, 1), pltpu.roll(flat, 128 - 80, 1))
    )
    lane = lax.broadcasted_iota(jnp.int32, (8, 128), 1)
    tiles = sep.shape[3] // 128
    full = [[jnp.zeros((8, 128), jnp.float32) for _ in range(tiles)] for _ in range(5)]
    for src in range(got.shape[0]):
        xl, xh, y, c = src // 32, src // 16 % 2, src // 2 % 8, src % 2
        block = flat[8 * src : 8 * src + 8]
        start = part * ((c * 2 + xl) * NY + y)
        for at in range(2 + xh):
            moved = pltpu.roll(block, (start - part * at) % 128, 1)
            to = 2 * xh + at
            for tile in range(start // 128, (start + part - 1) // 128 + 1):
                at_lane = lane + 128 * tile
                here = (at_lane >= start) & (at_lane < start + part)
                full[to][tile] = jnp.where(here, moved, full[to][tile])
    for tile in range(tiles):
        lanes = slice(128 * tile, 128 * (tile + 1))
        for k in range(4):
            sep[0, k, :, lanes] = full[k][tile]
        for layer in range(term.shape[0]):
            term[layer, :, lanes] = full[4][tile]


def in_hbm(array):
    return pltpu.with_memory_space_constraint(array, pltpu.HBM)


def in_vmem(array):
    return pltpu.with_memory_space_constraint(array, pltpu.VMEM)


def body(
    leaf_rhs,
    leaf_inverse,
    leaf_coupling,
    parent,
    sep_rhs,
    sep_inverse,
    sep_coupling,
    root_coupling,
    root_rhs,
    root_inverse,
):
    width, cols = leaf_coupling.shape[3], leaf_rhs.shape[3]
    part = cols // 32
    tiles = width // 128
    call = pl.pallas_call

    pack = call(
        pack_kernel,
        in_specs=[VMEM] * 5,
        out_specs=VMEM,
        out_shape=FLAT((NX, 5, 8, width), jnp.float32),
        name="pack",
    )(sep_inverse, sep_coupling, root_coupling, root_rhs, root_inverse)
    exchanged = lax.all_to_all(pack, X, 0, 0)

    leaf_rhs, leaf_inverse, leaf_coupling, sep_rhs = map(
        in_hbm, (leaf_rhs, leaf_inverse, leaf_coupling, sep_rhs)
    )
    send, xt, own = leaves_send(parent, leaf_rhs, leaf_inverse, leaf_coupling, sep_rhs)
    exchanged, xt = lax.optimization_barrier((exchanged, xt))
    weights = lax.all_gather(exchanged, ("y", "c"))
    keep = leaves_keep(parent, xt, own, leaf_coupling)
    res = keep + lax.ppermute(send, "c", [(0, 1), (1, 0)])
    res = lax.all_to_all(res.reshape(NX, 2 * tiles * 8 * part, 128), X, 0, 0)
    res = call(
        sum_kernel,
        in_specs=[VMEM],
        out_specs=VMEM,
        out_shape=FLAT((8, 2 * tiles * part, 128), jnp.float32),
        compiler_params=pltpu.CompilerParams(vmem_limit_bytes=16 * 2**20),
        name="sum_x",
    )(res)
    res = lax.all_to_all(res, "y", 0, 0)

    held, send, high, low = call(
        functools.partial(first_kernel, part),
        in_specs=[VMEM, HBM],
        out_specs=[VMEM] * 4,
        out_shape=[FLAT((2, 16, width), jnp.float32)] * 2 + [FLAT((3, width, width), jnp.bfloat16)] * 2,
        scratch_shapes=[pltpu.VMEM((5, 64, 8, width), jnp.float32), pltpu.SemaphoreType.DMA((5, NX))],
        compiler_params=pltpu.CompilerParams(vmem_limit_bytes=32 * 2**20),
        name="chain_first",
    )(res, in_hbm(weights))
    came = lax.ppermute(send, "xh", [(0, 1)])
    out = call(
        functools.partial(second_kernel, part),
        in_specs=[VMEM] * 4,
        out_specs=VMEM,
        out_shape=pltpu.VMEM((64, 3, 128), jnp.float32),
        scratch_shapes=[pltpu.VMEM((128, width), jnp.float32)],
        compiler_params=pltpu.CompilerParams(vmem_limit_bytes=16 * 2**20),
        name="chain_second",
    )(held, came, high, low)

    out = lax.all_to_all(out, ROW, 0, 0)
    sep_out, term = call(
        functools.partial(unpack_kernel, part),
        in_specs=[VMEM],
        out_specs=[VMEM] * 2,
        out_shape=[FLAT((1, 4, 8, cols), jnp.float32), pltpu.VMEM((8, 8, cols), jnp.float32)],
        scratch_shapes=[pltpu.VMEM((64 * 8, 128), jnp.float32)],
        name="unpack",
    )(in_vmem(out))
    root_out = lax.all_to_all(term, "layer", 0, 0).sum(0)
    return (sep_out, root_out)


def solution(mesh):
    fine = Mesh(mesh.devices.reshape(-1, 2, 2, NY, NC), ("layer",) + ROW)
    return jax.shard_map(
        body,
        mesh=fine,
        in_specs=(
            P("layer", ROW, None, None),
            P("layer", ROW, None, None),
            P("layer", ROW, None, None, None),
            P("layer", ROW),
            P("layer", None, ROW, None),
            P("layer", None, ROW, None),
            P("layer", None, ROW, None),
            P("layer", ROW, None),
            P(ROW, None),
            P(ROW, None),
        ),
        out_specs=(P("layer", None, ROW, None), P(ROW, None)),
        check_vma=False,
    )
```

```python
import functools

import jax
import jax.numpy as jnp
from jax import lax
from jax.experimental import pallas as pl
from jax.experimental.pallas import tpu as pltpu
from jax.sharding import Mesh, PartitionSpec as P

ROW = ("xl", "xh", "y", "c")
X = ("xl", "xh")
NX, NY, NC = 4, 8, 2
NT = (((1,), (1,)), ((), ()))
NN = (((1,), (0,)), ((), ()))
VMEM = pl.BlockSpec(memory_space=pltpu.VMEM)
SMEM = pl.BlockSpec(memory_space=pltpu.SMEM)
HBM = pl.BlockSpec(memory_space=pltpu.HBM)
FLAT = jax.ShapeDtypeStruct


def split(a):
    high = a.astype(jnp.bfloat16)
    return high, (a - high.astype(jnp.float32)).astype(jnp.bfloat16)


def stack(a):
    return jnp.concatenate(split(a), axis=0)


def dot3(a, b, dims):
    mm = functools.partial(lax.dot_general, dimension_numbers=dims, preferred_element_type=jnp.float32)
    rows = a.shape[0] // 2
    both = mm(a, b[0])
    return both[:rows] + (both[rows:] + mm(a[:rows], b[1]))


def pad(a):
    return jnp.concatenate([a, jnp.zeros((16 - a.shape[0], a.shape[1]), jnp.float32)], axis=0)


def by_tiles(ref, part):
    tiles, rows, _ = ref.shape

    def column(tile):
        return jnp.concatenate(
            [
                ref[tile, pl.ds(block + t, 8, stride=part), :]
                for block in range(0, rows, 8 * part)
                for t in range(part)
            ],
            axis=0,
        )

    return jnp.concatenate([column(tile) for tile in range(tiles)], axis=1)


def place():
    x = 2 * lax.axis_index("xl") + lax.axis_index("xh")
    return x, (x * NY + lax.axis_index("y")) * NC + lax.axis_index("c")


def pack_kernel(sep_inverse, sep_coupling, root_coupling, root_rhs, root_inverse, out, sems):
    tables = (
        [sep_inverse.at[0, 0], sep_inverse.at[0, 1], sep_coupling.at[0, 0], sep_coupling.at[0, 1], root_rhs],
        [sep_inverse.at[0, 2], sep_inverse.at[0, 3], sep_coupling.at[0, 2], root_coupling.at[0], root_inverse],
    )
    copies = []
    for x in range(out.shape[0]):
        for m, source in enumerate(tables[x % 2]):
            target = out.at[x, m, :, pl.ds(0, source.shape[1])]
            copies.append(pltpu.make_async_copy(source, target, sems.at[x, m]))
    for copy in copies:
        copy.start()
    for copy in copies:
        copy.wait()


def half_update(part, other, parent, xt, own, coupling, out, pair):
    k = pl.program_id(0)
    core = lax.axis_index("c")
    count = xt.shape[0] // NC
    half = pl.ds(pl.multiple_of((1 - core if other else core) * count, 64), count)

    @pl.when(k == 0)
    def _():
        pair[...] = stack(xt[half, :])

    keep = jnp.where(k >= parent[0, 0], 1.0, 0.0)
    got = dot3(pair[...], split(coupling[0, 0, 0]), NT) * -keep
    block = place()[1]
    first = 8 * (block % 16)
    mine = pltpu.roll(own[half, :], (first - 8 * k + 128) % 128, 1)
    lane = lax.broadcasted_iota(jnp.int32, mine.shape, 1)
    mine = jnp.where((lane >= first) & (lane < first + 8), mine, 0.0)
    group = 8 * part
    for side in range(2):
        rows = slice(side * group, (side + 1) * group)
        for tile in range(out.shape[3]):
            out[side, 0, 0, tile] = got[rows, 128 * tile : 128 * (tile + 1)]
        out[side, 0, 0, block // 16] += mine[rows]


def send_kernel(part, parent, rhs, inv, sep, coupling, out, xt, own, plain, tall, flat, *scratch):
    @pl.when(pl.program_id(0) == 0)
    def _():
        solved = dot3(stack(inv[0, 0]), split(rhs[0, 0]), NN).T
        for tile in range(plain.shape[0]):
            plain[tile] = solved[:, 128 * tile : 128 * (tile + 1)]
        xt[...] = by_tiles(plain, part)
        tall[...] = jnp.zeros_like(tall)
        for k in range(sep.shape[1]):
            tall[8 * k : 8 * k + 8, :] = sep[0, k]
        flat[0] = tall[...].T
        own[...] = by_tiles(flat, part)

    half_update(part, True, parent, xt, own, coupling, out, *scratch)


def keep_kernel(part, parent, xt, own, coupling, out, *scratch):
    half_update(part, False, parent, xt, own, coupling, out, *scratch)


def leaf_specs(coupling, cols):
    n, width, leaf = coupling.shape[2:]
    part, tiles = cols // 32, width // 128
    one = lambda *shape: pl.BlockSpec(shape, lambda k: (0,) * len(shape))
    coupling_spec = pl.BlockSpec((1, 1, 1, width, leaf), lambda k: (0, 0, k, 0, 0))
    half_spec = pl.BlockSpec((2, 1, 1, tiles, 8 * part, 128), lambda k: (0, k // 2, k % 2, 0, 0, 0))
    half_shape = FLAT((2, 2, 2, tiles, 8 * part, 128), jnp.float32)
    shared = [one(cols, leaf), one(cols, 128)]
    pair = pltpu.VMEM((2 * (cols // NC), leaf), jnp.bfloat16)
    params = pltpu.CompilerParams(vmem_limit_bytes=24 * 2**20)
    return part, one, coupling_spec, half_spec, half_shape, shared, pair, params


def leaves_send(parent, rhs, inv, coupling, sep):
    n, leaf, cols = coupling.shape[2], rhs.shape[2], rhs.shape[3]
    part, one, coupling_spec, half_spec, half_shape, shared, pair, params = leaf_specs(coupling, cols)
    return pl.pallas_call(
        functools.partial(send_kernel, part),
        grid=(n,),
        in_specs=[SMEM, one(1, 1, leaf, cols), one(1, 1, leaf, leaf), one(1, n, 8, cols), coupling_spec],
        out_specs=[half_spec] + shared,
        out_shape=[half_shape, FLAT((cols, leaf), jnp.float32), FLAT((cols, 128), jnp.float32)],
        scratch_shapes=[
            pltpu.VMEM((leaf // 128, cols, 128), jnp.float32),
            pltpu.VMEM((128, cols), jnp.float32),
            pltpu.VMEM((1, cols, 128), jnp.float32),
            pair,
        ],
        compiler_params=params,
        name="leaves_send",
    )(parent, rhs, inv, sep, coupling)


def leaves_keep(parent, xt, own, coupling):
    part, _, coupling_spec, half_spec, half_shape, shared, pair, params = leaf_specs(coupling, xt.shape[0])
    return pl.pallas_call(
        functools.partial(keep_kernel, part),
        grid=(coupling.shape[2],),
        in_specs=[SMEM] + shared + [coupling_spec],
        out_specs=half_spec,
        out_shape=half_shape,
        scratch_shapes=[pair],
        compiler_params=params,
        name="leaves_keep",
    )(parent, xt, own, coupling)


def sum_kernel(parts, out):
    count = out.shape[1]
    for s in range(8):
        rows = pl.ds(s, count, stride=8)
        out[s] = (parts[0, rows, :] + parts[1, rows, :]) + (parts[2, rows, :] + parts[3, rows, :])


def first_kernel(part, cols, parts, weights, held, send, high, low, full, sems):
    odd = lax.axis_index("xh") == 1

    def copies(m):
        return [
            pltpu.make_async_copy(
                weights.at[:, src, m], full.at[m, pl.ds(16 * src, 16)], sems.at[m, src]
            )
            for src in range(NX)
        ]

    def matrix(m):
        for copy in copies(m):
            copy.wait()
        return split(full[m].reshape(-1, full.shape[3]))

    for m in range(full.shape[0]):
        for copy in copies(m):
            copy.start()

    res = parts[0]
    for p in range(1, parts.shape[0]):
        res = res + parts[p]
    tiles = res.shape[0] // (2 * part)

    def residual(k):
        starts = [part * (tiles * k + tile) for tile in range(tiles)]
        rows = jnp.concatenate([res[at : at + part] for at in starts], axis=1)
        return stack(pad(rows))

    first = dot3(residual(0), matrix(0), NT)
    second = dot3(residual(1), matrix(1), NT)
    held[0] = first
    held[1] = second

    @pl.when(jnp.logical_not(odd))
    def _():
        chained = second - dot3(stack(first), matrix(2), NT)
        held[1] = chained
        send[:part] = dot3(stack(chained), matrix(3), NT)[:part]
        shape = (16, cols)
        group = (lax.axis_index("c") * 2 + lax.axis_index("xl")) * NY + lax.axis_index("y")
        column = lax.broadcasted_iota(jnp.int32, shape, 0) + part * group
        mine = lax.broadcasted_iota(jnp.int32, shape, 1) == column
        pick = jnp.where(mine, jnp.where(lax.axis_index("layer") == 0, 1.0, 0.0), 0.0).astype(jnp.bfloat16)
        mm = functools.partial(lax.dot_general, dimension_numbers=NT, preferred_element_type=jnp.float32)
        rhs_high, rhs_low = (half[:, :cols] for half in matrix(4))
        send[part:] = (mm(pick, rhs_high) + mm(pick, rhs_low))[:part]

    @pl.when(odd)
    def _():
        for m in range(2, full.shape[0]):
            high[m - 2], low[m - 2] = matrix(m)


def second_kernel(part, held, came, high, low, out, wide):
    wide[...] = jnp.zeros_like(wide)
    step = 40

    def store(at, value):
        for copy in range(3):
            wide[step * copy + part * at : step * copy + part * (at + 1), :] = value[:part]

    @pl.when(lax.axis_index("xh") == 0)
    def _():
        store(0, held[0])
        store(1, held[1])

    @pl.when(lax.axis_index("xh") == 1)
    def _():
        third = pad(held[0, :part] - came[:part])
        store(0, third)
        fourth = held[1] - dot3(stack(third), (high[0], low[0]), NT)
        store(1, fourth)
        term = came[part:] - dot3(stack(fourth), (high[1], low[1]), NT)[:part]
        store(2, dot3(stack(pad(term)), (high[2], low[2]), NT))

    rows = wide[...].T.reshape(-1, 8, 128)
    lane = lax.broadcasted_iota(jnp.int32, (rows.shape[0], 1, 128), 2)
    for j in range(3):
        far = min(6 + j, 7)
        low_rows = jnp.where(lane < 80, rows[:, 3 + j : 4 + j], rows[:, far : far + 1])
        out[:, j : j + 1, :] = jnp.where(lane < 40, rows[:, j : j + 1], low_rows)


def unpack_kernel(part, got, sep, term, tall):
    for src in range(got.shape[0]):
        tall[8 * src : 8 * src + 3, :] = got[src]
        tall[8 * src + 3 : 8 * src + 6, :] = got[src]
        tall[8 * src + 6 : 8 * src + 8, :] = got[src, 0:2]
    flat = tall[...]
    row = lax.broadcasted_iota(jnp.int32, flat.shape, 0) % 8
    flat = jnp.where(
        row < 3, flat, jnp.where(row < 6, pltpu.roll(flat, 128 - 40, 1), pltpu.roll(flat, 128 - 80, 1))
    )
    lane = lax.broadcasted_iota(jnp.int32, (8, 128), 1)
    tiles = sep.shape[3] // 128
    full = [[jnp.zeros((8, 128), jnp.float32) for _ in range(tiles)] for _ in range(5)]
    for src in range(got.shape[0]):
        xl, xh, y, c = src // 32, src // 16 % 2, src // 2 % 8, src % 2
        block = flat[8 * src : 8 * src + 8]
        start = part * ((c * 2 + xl) * NY + y)
        for at in range(2 + xh):
            moved = pltpu.roll(block, (start - part * at) % 128, 1)
            to = 2 * xh + at
            for tile in range(start // 128, (start + part - 1) // 128 + 1):
                at_lane = lane + 128 * tile
                here = (at_lane >= start) & (at_lane < start + part)
                full[to][tile] = jnp.where(here, moved, full[to][tile])
    for tile in range(tiles):
        lanes = slice(128 * tile, 128 * (tile + 1))
        for k in range(4):
            sep[0, k, :, lanes] = full[k][tile]
        for layer in range(term.shape[0]):
            term[layer, :, lanes] = full[4][tile]


def in_hbm(array):
    return pltpu.with_memory_space_constraint(array, pltpu.HBM)


def in_vmem(array):
    return pltpu.with_memory_space_constraint(array, pltpu.VMEM)


def body(
    leaf_rhs,
    leaf_inverse,
    leaf_coupling,
    parent,
    sep_rhs,
    sep_inverse,
    sep_coupling,
    root_coupling,
    root_rhs,
    root_inverse,
):
    width, cols = leaf_coupling.shape[3], leaf_rhs.shape[3]
    part = cols // 32
    tiles = width // 128
    call = pl.pallas_call

    pack = call(
        pack_kernel,
        in_specs=[HBM] * 5,
        out_specs=HBM,
        out_shape=pltpu.HBM((NX, 5, 8, width), jnp.float32),
        scratch_shapes=[pltpu.SemaphoreType.DMA((NX, 5))],
        name="pack",
    )(*map(in_hbm, (sep_inverse, sep_coupling, root_coupling, root_rhs, root_inverse)))
    exchanged = lax.all_to_all(pack, X, 0, 0)

    leaf_rhs, leaf_inverse, leaf_coupling, sep_rhs = map(
        in_hbm, (leaf_rhs, leaf_inverse, leaf_coupling, sep_rhs)
    )
    send, xt, own = leaves_send(parent, leaf_rhs, leaf_inverse, leaf_coupling, sep_rhs)
    exchanged, xt = lax.optimization_barrier((exchanged, xt))
    weights = lax.all_gather(exchanged, ("y", "c"))
    keep = leaves_keep(parent, xt, own, leaf_coupling)
    res = keep + lax.ppermute(send, "c", [(0, 1), (1, 0)])
    res = lax.all_to_all(res.reshape(NX, 2 * tiles * 8 * part, 128), X, 0, 0)
    res = call(
        sum_kernel,
        in_specs=[VMEM],
        out_specs=VMEM,
        out_shape=FLAT((8, 2 * tiles * part, 128), jnp.float32),
        compiler_params=pltpu.CompilerParams(vmem_limit_bytes=16 * 2**20),
        name="sum_x",
    )(res)
    res = lax.all_to_all(res, "y", 0, 0)

    held, send, high, low = call(
        functools.partial(first_kernel, part, cols),
        in_specs=[VMEM, HBM],
        out_specs=[VMEM] * 4,
        out_shape=[FLAT((2, 16, width), jnp.float32), FLAT((2 * part, width), jnp.float32)]
        + [FLAT((3, width, width), jnp.bfloat16)] * 2,
        scratch_shapes=[pltpu.VMEM((5, 64, 8, width), jnp.float32), pltpu.SemaphoreType.DMA((5, NX))],
        compiler_params=pltpu.CompilerParams(vmem_limit_bytes=32 * 2**20),
        name="chain_first",
    )(res, in_hbm(weights))
    came = lax.ppermute(send, "xh", [(0, 1)])
    out = call(
        functools.partial(second_kernel, part),
        in_specs=[VMEM] * 4,
        out_specs=VMEM,
        out_shape=pltpu.VMEM((64, 3, 128), jnp.float32),
        scratch_shapes=[pltpu.VMEM((128, width), jnp.float32)],
        compiler_params=pltpu.CompilerParams(vmem_limit_bytes=16 * 2**20),
        name="chain_second",
    )(held, came, high, low)

    out = lax.all_to_all(out, ROW, 0, 0)
    sep_out, term = call(
        functools.partial(unpack_kernel, part),
        in_specs=[VMEM],
        out_specs=[VMEM] * 2,
        out_shape=[FLAT((1, 4, 8, cols), jnp.float32), pltpu.VMEM((8, 8, cols), jnp.float32)],
        scratch_shapes=[pltpu.VMEM((64 * 8, 128), jnp.float32)],
        name="unpack",
    )(in_vmem(out))
    root_out = lax.all_to_all(term, "layer", 0, 0).sum(0)
    return (sep_out, root_out)


def solution(mesh):
    fine = Mesh(mesh.devices.reshape(-1, 2, 2, NY, NC), ("layer",) + ROW)
    return jax.shard_map(
        body,
        mesh=fine,
        in_specs=(
            P("layer", ROW, None, None),
            P("layer", ROW, None, None),
            P("layer", ROW, None, None, None),
            P("layer", ROW),
            P("layer", None, ROW, None),
            P("layer", None, ROW, None),
            P("layer", None, ROW, None),
            P("layer", ROW, None),
            P(ROW, None),
            P(ROW, None),
        ),
        out_specs=(P("layer", None, ROW, None), P(ROW, None)),
        check_vma=False,
    )
```

```python
import functools

import jax
import jax.numpy as jnp
from jax import lax
from jax.experimental import pallas as pl
from jax.experimental.pallas import tpu as pltpu
from jax.sharding import Mesh, PartitionSpec as P

ROW = ("xl", "xh", "y", "c")
X = ("xl", "xh")
NX, NY, NC = 4, 8, 2
NT = (((1,), (1,)), ((), ()))
NN = (((1,), (0,)), ((), ()))
VMEM = pl.BlockSpec(memory_space=pltpu.VMEM)
SMEM = pl.BlockSpec(memory_space=pltpu.SMEM)
HBM = pl.BlockSpec(memory_space=pltpu.HBM)
FLAT = jax.ShapeDtypeStruct


def split(a):
    high = a.astype(jnp.bfloat16)
    return high, (a - high.astype(jnp.float32)).astype(jnp.bfloat16)


def stack(a):
    return jnp.concatenate(split(a), axis=0)


def dot3(a, b, dims):
    mm = functools.partial(lax.dot_general, dimension_numbers=dims, preferred_element_type=jnp.float32)
    rows = a.shape[0] // 2
    both = mm(a, b[0])
    return both[:rows] + (both[rows:] + mm(a[:rows], b[1]))


def pad(a):
    return jnp.concatenate([a, jnp.zeros((16 - a.shape[0], a.shape[1]), jnp.float32)], axis=0)


def by_tiles(ref, part):
    tiles, rows, _ = ref.shape

    def column(tile):
        return jnp.concatenate(
            [
                ref[tile, pl.ds(block + t, 8, stride=part), :]
                for block in range(0, rows, 8 * part)
                for t in range(part)
            ],
            axis=0,
        )

    return jnp.concatenate([column(tile) for tile in range(tiles)], axis=1)


def place():
    x = 2 * lax.axis_index("xl") + lax.axis_index("xh")
    return x, (x * NY + lax.axis_index("y")) * NC + lax.axis_index("c")


def pack_kernel(sep_inverse, sep_coupling, root_coupling, root_rhs, root_inverse, out):
    zeros = jnp.zeros_like(root_inverse)
    rr = jnp.concatenate([root_rhs[...], zeros[:, root_rhs.shape[1] :]], axis=1)
    tables = (
        [sep_inverse[0, 0], sep_inverse[0, 1], sep_coupling[0, 0], sep_coupling[0, 1], rr],
        [sep_inverse[0, 2], sep_inverse[0, 3], sep_coupling[0, 2], root_coupling[0], root_inverse[...]],
    )
    for x in range(out.shape[0]):
        for m in range(out.shape[1]):
            out[x, m] = tables[x % 2][m]


def half_update(part, other, parent, xt, own, coupling, out, pair):
    k = pl.program_id(0)
    core = lax.axis_index("c")
    count = xt.shape[0] // NC
    half = pl.ds(pl.multiple_of((1 - core if other else core) * count, 64), count)

    @pl.when(k == 0)
    def _():
        pair[...] = stack(xt[half, :])

    keep = jnp.where(k >= parent[0, 0], 1.0, 0.0)
    got = dot3(pair[...], split(coupling[0, 0, 0]), NT) * -keep
    block = place()[1]
    first = 8 * (block % 16)
    mine = pltpu.roll(own[half, :], (first - 8 * k + 128) % 128, 1)
    lane = lax.broadcasted_iota(jnp.int32, mine.shape, 1)
    mine = jnp.where((lane >= first) & (lane < first + 8), mine, 0.0)
    group = 8 * part
    for side in range(2):
        rows = slice(side * group, (side + 1) * group)
        for tile in range(out.shape[3]):
            out[side, 0, 0, tile] = got[rows, 128 * tile : 128 * (tile + 1)]
        out[side, 0, 0, block // 16] += mine[rows]


def send_kernel(part, parent, rhs, inv, sep, coupling, out, xt, own, plain, tall, flat, *scratch):
    @pl.when(pl.program_id(0) == 0)
    def _():
        solved = dot3(stack(inv[0, 0]), split(rhs[0, 0]), NN).T
        for tile in range(plain.shape[0]):
            plain[tile] = solved[:, 128 * tile : 128 * (tile + 1)]
        xt[...] = by_tiles(plain, part)
        tall[...] = jnp.zeros_like(tall)
        for k in range(sep.shape[1]):
            tall[8 * k : 8 * k + 8, :] = sep[0, k]
        flat[0] = tall[...].T
        own[...] = by_tiles(flat, part)

    half_update(part, True, parent, xt, own, coupling, out, *scratch)


def keep_kernel(part, parent, xt, own, coupling, out, *scratch):
    half_update(part, False, parent, xt, own, coupling, out, *scratch)


def leaf_specs(coupling, cols):
    n, width, leaf = coupling.shape[2:]
    part, tiles = cols // 32, width // 128
    one = lambda *shape: pl.BlockSpec(shape, lambda k: (0,) * len(shape))
    coupling_spec = pl.BlockSpec((1, 1, 1, width, leaf), lambda k: (0, 0, k, 0, 0))
    half_spec = pl.BlockSpec((2, 1, 1, tiles, 8 * part, 128), lambda k: (0, k // 2, k % 2, 0, 0, 0))
    half_shape = FLAT((2, 2, 2, tiles, 8 * part, 128), jnp.float32)
    shared = [one(cols, leaf), one(cols, 128)]
    pair = pltpu.VMEM((2 * (cols // NC), leaf), jnp.bfloat16)
    params = pltpu.CompilerParams(vmem_limit_bytes=24 * 2**20)
    return part, one, coupling_spec, half_spec, half_shape, shared, pair, params


def leaves_send(parent, rhs, inv, coupling, sep):
    n, leaf, cols = coupling.shape[2], rhs.shape[2], rhs.shape[3]
    part, one, coupling_spec, half_spec, half_shape, shared, pair, params = leaf_specs(coupling, cols)
    return pl.pallas_call(
        functools.partial(send_kernel, part),
        grid=(n,),
        in_specs=[SMEM, one(1, 1, leaf, cols), one(1, 1, leaf, leaf), one(1, n, 8, cols), coupling_spec],
        out_specs=[half_spec] + shared,
        out_shape=[half_shape, FLAT((cols, leaf), jnp.float32), FLAT((cols, 128), jnp.float32)],
        scratch_shapes=[
            pltpu.VMEM((leaf // 128, cols, 128), jnp.float32),
            pltpu.VMEM((128, cols), jnp.float32),
            pltpu.VMEM((1, cols, 128), jnp.float32),
            pair,
        ],
        compiler_params=params,
        name="leaves_send",
    )(parent, rhs, inv, sep, coupling)


def leaves_keep(parent, xt, own, coupling):
    part, _, coupling_spec, half_spec, half_shape, shared, pair, params = leaf_specs(coupling, xt.shape[0])
    return pl.pallas_call(
        functools.partial(keep_kernel, part),
        grid=(coupling.shape[2],),
        in_specs=[SMEM] + shared + [coupling_spec],
        out_specs=half_spec,
        out_shape=half_shape,
        scratch_shapes=[pair],
        compiler_params=params,
        name="leaves_keep",
    )(parent, xt, own, coupling)


def sum_kernel(parts, out):
    count = out.shape[1]
    for s in range(8):
        rows = pl.ds(s, count, stride=8)
        out[s] = (parts[0, rows, :] + parts[1, rows, :]) + (parts[2, rows, :] + parts[3, rows, :])


def first_kernel(part, cols, parts, weights, held, send, high, low, full, sems):
    odd = lax.axis_index("xh") == 1

    def copies(m):
        return [
            pltpu.make_async_copy(
                weights.at[:, src, m], full.at[m, pl.ds(16 * src, 16)], sems.at[m, src]
            )
            for src in range(NX)
        ]

    def matrix(m):
        for copy in copies(m):
            copy.wait()
        return split(full[m].reshape(-1, full.shape[3]))

    for m in range(full.shape[0]):
        for copy in copies(m):
            copy.start()

    res = parts[0]
    for p in range(1, parts.shape[0]):
        res = res + parts[p]
    tiles = res.shape[0] // (2 * part)

    def residual(k):
        starts = [part * (tiles * k + tile) for tile in range(tiles)]
        rows = jnp.concatenate([res[at : at + part] for at in starts], axis=1)
        return stack(pad(rows))

    first = dot3(residual(0), matrix(0), NT)
    second = dot3(residual(1), matrix(1), NT)
    held[0] = first
    held[1] = second

    @pl.when(jnp.logical_not(odd))
    def _():
        chained = second - dot3(stack(first), matrix(2), NT)
        held[1] = chained
        send[:part] = dot3(stack(chained), matrix(3), NT)[:part]
        shape = (16, cols)
        group = (lax.axis_index("c") * 2 + lax.axis_index("xl")) * NY + lax.axis_index("y")
        column = lax.broadcasted_iota(jnp.int32, shape, 0) + part * group
        mine = lax.broadcasted_iota(jnp.int32, shape, 1) == column
        pick = jnp.where(mine, jnp.where(lax.axis_index("layer") == 0, 1.0, 0.0), 0.0).astype(jnp.bfloat16)
        mm = functools.partial(lax.dot_general, dimension_numbers=NT, preferred_element_type=jnp.float32)
        rhs_high, rhs_low = (half[:, :cols] for half in matrix(4))
        send[part:] = (mm(pick, rhs_high) + mm(pick, rhs_low))[:part]

    @pl.when(odd)
    def _():
        for m in range(2, full.shape[0]):
            high[m - 2], low[m - 2] = matrix(m)


def second_kernel(part, held, came, high, low, out, wide):
    wide[...] = jnp.zeros_like(wide)
    step = 40

    def store(at, value):
        for copy in range(3):
            wide[step * copy + part * at : step * copy + part * (at + 1), :] = value[:part]

    @pl.when(lax.axis_index("xh") == 0)
    def _():
        store(0, held[0])
        store(1, held[1])

    @pl.when(lax.axis_index("xh") == 1)
    def _():
        third = pad(held[0, :part] - came[:part])
        store(0, third)
        fourth = held[1] - dot3(stack(third), (high[0], low[0]), NT)
        store(1, fourth)
        term = came[part:] - dot3(stack(fourth), (high[1], low[1]), NT)[:part]
        store(2, dot3(stack(pad(term)), (high[2], low[2]), NT))

    rows = wide[...].T.reshape(-1, 8, 128)
    lane = lax.broadcasted_iota(jnp.int32, (rows.shape[0], 1, 128), 2)
    for j in range(3):
        far = min(6 + j, 7)
        low_rows = jnp.where(lane < 80, rows[:, 3 + j : 4 + j], rows[:, far : far + 1])
        out[:, j : j + 1, :] = jnp.where(lane < 40, rows[:, j : j + 1], low_rows)


def unpack_kernel(part, got, sep, term, tall):
    for src in range(got.shape[0]):
        tall[8 * src : 8 * src + 3, :] = got[src]
        tall[8 * src + 3 : 8 * src + 6, :] = got[src]
        tall[8 * src + 6 : 8 * src + 8, :] = got[src, 0:2]
    flat = tall[...]
    row = lax.broadcasted_iota(jnp.int32, flat.shape, 0) % 8
    flat = jnp.where(
        row < 3, flat, jnp.where(row < 6, pltpu.roll(flat, 128 - 40, 1), pltpu.roll(flat, 128 - 80, 1))
    )
    lane = lax.broadcasted_iota(jnp.int32, (8, 128), 1)
    tiles = sep.shape[3] // 128
    full = [[jnp.zeros((8, 128), jnp.float32) for _ in range(tiles)] for _ in range(5)]
    for src in range(got.shape[0]):
        xl, xh, y, c = src // 32, src // 16 % 2, src // 2 % 8, src % 2
        block = flat[8 * src : 8 * src + 8]
        start = part * ((c * 2 + xl) * NY + y)
        for at in range(2 + xh):
            moved = pltpu.roll(block, (start - part * at) % 128, 1)
            to = 2 * xh + at
            for tile in range(start // 128, (start + part - 1) // 128 + 1):
                at_lane = lane + 128 * tile
                here = (at_lane >= start) & (at_lane < start + part)
                full[to][tile] = jnp.where(here, moved, full[to][tile])
    for tile in range(tiles):
        lanes = slice(128 * tile, 128 * (tile + 1))
        for k in range(4):
            sep[0, k, :, lanes] = full[k][tile]
        for layer in range(term.shape[0]):
            term[layer, :, lanes] = full[4][tile]


def in_hbm(array):
    return pltpu.with_memory_space_constraint(array, pltpu.HBM)


def in_vmem(array):
    return pltpu.with_memory_space_constraint(array, pltpu.VMEM)


def body(
    leaf_rhs,
    leaf_inverse,
    leaf_coupling,
    parent,
    sep_rhs,
    sep_inverse,
    sep_coupling,
    root_coupling,
    root_rhs,
    root_inverse,
):
    width, cols = leaf_coupling.shape[3], leaf_rhs.shape[3]
    part = cols // 32
    tiles = width // 128
    call = pl.pallas_call

    pack = call(
        pack_kernel,
        in_specs=[VMEM] * 5,
        out_specs=VMEM,
        out_shape=pltpu.VMEM((NX, 5, 8, width), jnp.float32),
        name="pack",
    )(sep_inverse, sep_coupling, root_coupling, root_rhs, root_inverse)
    exchanged = lax.all_to_all(pack, X, 0, 0)

    leaf_rhs, leaf_inverse, leaf_coupling, sep_rhs = map(
        in_hbm, (leaf_rhs, leaf_inverse, leaf_coupling, sep_rhs)
    )
    send, xt, own = leaves_send(parent, leaf_rhs, leaf_inverse, leaf_coupling, sep_rhs)
    exchanged, xt = lax.optimization_barrier((exchanged, xt))
    weights = lax.all_gather(exchanged, ("y", "c"))
    keep = leaves_keep(parent, xt, own, leaf_coupling)
    res = keep + lax.ppermute(send, "c", [(0, 1), (1, 0)])
    res = lax.all_to_all(res.reshape(NX, 2 * tiles * 8 * part, 128), X, 0, 0)
    res = call(
        sum_kernel,
        in_specs=[VMEM],
        out_specs=VMEM,
        out_shape=FLAT((8, 2 * tiles * part, 128), jnp.float32),
        compiler_params=pltpu.CompilerParams(vmem_limit_bytes=16 * 2**20),
        name="sum_x",
    )(res)
    res = lax.all_to_all(res, "y", 0, 0)

    held, send, high, low = call(
        functools.partial(first_kernel, part, cols),
        in_specs=[VMEM, HBM],
        out_specs=[VMEM] * 4,
        out_shape=[FLAT((2, 16, width), jnp.float32), FLAT((2 * part, width), jnp.float32)]
        + [FLAT((3, width, width), jnp.bfloat16)] * 2,
        scratch_shapes=[pltpu.VMEM((5, 64, 8, width), jnp.float32), pltpu.SemaphoreType.DMA((5, NX))],
        compiler_params=pltpu.CompilerParams(vmem_limit_bytes=32 * 2**20),
        name="chain_first",
    )(res, in_hbm(weights))
    came = lax.ppermute(send, "xh", [(0, 1)])
    out = call(
        functools.partial(second_kernel, part),
        in_specs=[VMEM] * 4,
        out_specs=VMEM,
        out_shape=pltpu.VMEM((64, 3, 128), jnp.float32),
        scratch_shapes=[pltpu.VMEM((128, width), jnp.float32)],
        compiler_params=pltpu.CompilerParams(vmem_limit_bytes=16 * 2**20),
        name="chain_second",
    )(held, came, high, low)

    out = lax.all_to_all(out, ROW, 0, 0)
    sep_out, term = call(
        functools.partial(unpack_kernel, part),
        in_specs=[VMEM],
        out_specs=[VMEM] * 2,
        out_shape=[FLAT((1, 4, 8, cols), jnp.float32), pltpu.VMEM((8, 8, cols), jnp.float32)],
        scratch_shapes=[pltpu.VMEM((64 * 8, 128), jnp.float32)],
        name="unpack",
    )(in_vmem(out))
    root_out = lax.all_to_all(term, "layer", 0, 0).sum(0)
    return (sep_out, root_out)


def solution(mesh):
    fine = Mesh(mesh.devices.reshape(-1, 2, 2, NY, NC), ("layer",) + ROW)
    return jax.shard_map(
        body,
        mesh=fine,
        in_specs=(
            P("layer", ROW, None, None),
            P("layer", ROW, None, None),
            P("layer", ROW, None, None, None),
            P("layer", ROW),
            P("layer", None, ROW, None),
            P("layer", None, ROW, None),
            P("layer", None, ROW, None),
            P("layer", ROW, None),
            P(ROW, None),
            P(ROW, None),
        ),
        out_specs=(P("layer", None, ROW, None), P(ROW, None)),
        check_vma=False,
    )
```

```python
import functools

import jax
import jax.numpy as jnp
from jax import lax
from jax.experimental import pallas as pl
from jax.experimental.pallas import tpu as pltpu
from jax.sharding import Mesh, PartitionSpec as P

ROW = ("xl", "xh", "y", "c")
X = ("xl", "xh")
NX, NY, NC = 4, 8, 2
NT = (((1,), (1,)), ((), ()))
NN = (((1,), (0,)), ((), ()))
VMEM = pl.BlockSpec(memory_space=pltpu.VMEM)
SMEM = pl.BlockSpec(memory_space=pltpu.SMEM)
HBM = pl.BlockSpec(memory_space=pltpu.HBM)
FLAT = jax.ShapeDtypeStruct


def split(a):
    high = a.astype(jnp.bfloat16)
    return high, (a - high.astype(jnp.float32)).astype(jnp.bfloat16)


def stack(a):
    return jnp.concatenate(split(a), axis=0)


def dot3(a, b, dims):
    mm = functools.partial(lax.dot_general, dimension_numbers=dims, preferred_element_type=jnp.float32)
    rows = a.shape[0] // 2
    both = mm(a, b[0])
    return both[:rows] + (both[rows:] + mm(a[:rows], b[1]))


def pad(a):
    return jnp.concatenate([a, jnp.zeros((16 - a.shape[0], a.shape[1]), jnp.float32)], axis=0)


def by_tiles(ref, part):
    tiles, rows, _ = ref.shape

    def column(tile):
        return jnp.concatenate(
            [
                ref[tile, pl.ds(block + t, 8, stride=part), :]
                for block in range(0, rows, 8 * part)
                for t in range(part)
            ],
            axis=0,
        )

    return jnp.concatenate([column(tile) for tile in range(tiles)], axis=1)


def place():
    x = 2 * lax.axis_index("xl") + lax.axis_index("xh")
    return x, (x * NY + lax.axis_index("y")) * NC + lax.axis_index("c")


def pack_kernel(sep_inverse, sep_coupling, root_coupling, root_rhs, root_inverse, out):
    zeros = jnp.zeros_like(root_inverse)
    rr = jnp.concatenate([root_rhs[...], zeros[:, root_rhs.shape[1] :]], axis=1)
    tables = (
        [sep_inverse[0, 0], sep_inverse[0, 1], sep_coupling[0, 0], sep_coupling[0, 1], rr],
        [sep_inverse[0, 2], sep_inverse[0, 3], sep_coupling[0, 2], root_coupling[0], root_inverse[...]],
    )
    for x in range(out.shape[0]):
        for m in range(out.shape[1]):
            out[x, m] = tables[x % 2][m]


def half_update(part, other, parent, xt, own, coupling, out, pair):
    k = pl.program_id(0)
    core = lax.axis_index("c")
    count = xt.shape[0] // NC
    half = pl.ds(pl.multiple_of((1 - core if other else core) * count, 64), count)

    @pl.when(k == 0)
    def _():
        pair[...] = stack(xt[half, :])

    keep = jnp.where(k >= parent[0, 0], 1.0, 0.0)
    got = dot3(pair[...], split(coupling[0, 0, 0]), NT) * -keep
    block = place()[1]
    first = 8 * (block % 16)
    mine = pltpu.roll(own[half, :], (first - 8 * k + 128) % 128, 1)
    lane = lax.broadcasted_iota(jnp.int32, mine.shape, 1)
    mine = jnp.where((lane >= first) & (lane < first + 8), mine, 0.0)
    group = 8 * part
    for side in range(2):
        rows = slice(side * group, (side + 1) * group)
        for tile in range(out.shape[3]):
            out[side, 0, 0, tile] = got[rows, 128 * tile : 128 * (tile + 1)]
        out[side, 0, 0, block // 16] += mine[rows]


def send_kernel(part, parent, rhs, inv, sep, coupling, out, xt, own, plain, tall, flat, *scratch):
    @pl.when(pl.program_id(0) == 0)
    def _():
        solved = dot3(stack(inv[0, 0]), split(rhs[0, 0]), NN).T
        for tile in range(plain.shape[0]):
            plain[tile] = solved[:, 128 * tile : 128 * (tile + 1)]
        xt[...] = by_tiles(plain, part)
        tall[...] = jnp.zeros_like(tall)
        for k in range(sep.shape[1]):
            tall[8 * k : 8 * k + 8, :] = sep[0, k]
        flat[0] = tall[...].T
        own[...] = by_tiles(flat, part)

    half_update(part, True, parent, xt, own, coupling, out, *scratch)


def keep_kernel(part, parent, xt, own, coupling, out, *scratch):
    half_update(part, False, parent, xt, own, coupling, out, *scratch)


def leaf_specs(coupling, cols):
    n, width, leaf = coupling.shape[2:]
    part, tiles = cols // 32, width // 128
    one = lambda *shape: pl.BlockSpec(shape, lambda k: (0,) * len(shape))
    coupling_spec = pl.BlockSpec((1, 1, 1, width, leaf), lambda k: (0, 0, k, 0, 0))
    half_spec = pl.BlockSpec((2, 1, 1, tiles, 8 * part, 128), lambda k: (0, k // 2, k % 2, 0, 0, 0))
    half_shape = FLAT((2, 2, 2, tiles, 8 * part, 128), jnp.float32)
    shared = [one(cols, leaf), one(cols, 128)]
    pair = pltpu.VMEM((2 * (cols // NC), leaf), jnp.bfloat16)
    params = pltpu.CompilerParams(vmem_limit_bytes=24 * 2**20)
    return part, one, coupling_spec, half_spec, half_shape, shared, pair, params


def leaves_send(parent, rhs, inv, coupling, sep):
    n, leaf, cols = coupling.shape[2], rhs.shape[2], rhs.shape[3]
    part, one, coupling_spec, half_spec, half_shape, shared, pair, params = leaf_specs(coupling, cols)
    return pl.pallas_call(
        functools.partial(send_kernel, part),
        grid=(n,),
        in_specs=[SMEM, one(1, 1, leaf, cols), one(1, 1, leaf, leaf), one(1, n, 8, cols), coupling_spec],
        out_specs=[half_spec] + shared,
        out_shape=[half_shape, FLAT((cols, leaf), jnp.float32), FLAT((cols, 128), jnp.float32)],
        scratch_shapes=[
            pltpu.VMEM((leaf // 128, cols, 128), jnp.float32),
            pltpu.VMEM((128, cols), jnp.float32),
            pltpu.VMEM((1, cols, 128), jnp.float32),
            pair,
        ],
        compiler_params=params,
        name="leaves_send",
    )(parent, rhs, inv, sep, coupling)


def leaves_keep(parent, xt, own, coupling):
    part, _, coupling_spec, half_spec, half_shape, shared, pair, params = leaf_specs(coupling, xt.shape[0])
    return pl.pallas_call(
        functools.partial(keep_kernel, part),
        grid=(coupling.shape[2],),
        in_specs=[SMEM] + shared + [coupling_spec],
        out_specs=half_spec,
        out_shape=half_shape,
        scratch_shapes=[pair],
        compiler_params=params,
        name="leaves_keep",
    )(parent, xt, own, coupling)


def sum_kernel(parts, out):
    count = out.shape[1]
    for s in range(8):
        rows = pl.ds(s, count, stride=8)
        out[s] = (parts[0, rows, :] + parts[1, rows, :]) + (parts[2, rows, :] + parts[3, rows, :])


def first_kernel(part, cols, parts, weights, held, send, high, low, full, sems):
    odd = lax.axis_index("xh") == 1

    def copies(m):
        return [
            pltpu.make_async_copy(
                weights.at[pl.ds(NY * core, NY), src, m], full.at[m, src, :, core], sems.at[m, src, core]
            )
            for src in range(NX)
            for core in range(NC)
        ]

    def matrix(m):
        for copy in copies(m):
            copy.wait()
        return split(full[m].reshape(-1, full.shape[-1]))

    for m in range(full.shape[0]):
        for copy in copies(m):
            copy.start()

    res = parts[0]
    for p in range(1, parts.shape[0]):
        res = res + parts[p]
    tiles = res.shape[0] // (2 * part)

    def residual(k):
        starts = [part * (tiles * k + tile) for tile in range(tiles)]
        rows = jnp.concatenate([res[at : at + part] for at in starts], axis=1)
        return stack(pad(rows))

    first = dot3(residual(0), matrix(0), NT)
    second = dot3(residual(1), matrix(1), NT)
    held[0] = first
    held[1] = second

    @pl.when(jnp.logical_not(odd))
    def _():
        chained = second - dot3(stack(first), matrix(2), NT)
        held[1] = chained
        send[:part] = dot3(stack(chained), matrix(3), NT)[:part]
        shape = (16, cols)
        group = (lax.axis_index("c") * 2 + lax.axis_index("xl")) * NY + lax.axis_index("y")
        column = lax.broadcasted_iota(jnp.int32, shape, 0) + part * group
        mine = lax.broadcasted_iota(jnp.int32, shape, 1) == column
        pick = jnp.where(mine, jnp.where(lax.axis_index("layer") == 0, 1.0, 0.0), 0.0).astype(jnp.bfloat16)
        mm = functools.partial(lax.dot_general, dimension_numbers=NT, preferred_element_type=jnp.float32)
        rhs_high, rhs_low = (half[:, :cols] for half in matrix(4))
        send[part:] = (mm(pick, rhs_high) + mm(pick, rhs_low))[:part]

    @pl.when(odd)
    def _():
        for m in range(2, full.shape[0]):
            high[m - 2], low[m - 2] = matrix(m)


def second_kernel(part, held, came, high, low, out, wide):
    wide[...] = jnp.zeros_like(wide)
    step = 40

    def store(at, value):
        for copy in range(3):
            wide[step * copy + part * at : step * copy + part * (at + 1), :] = value[:part]

    @pl.when(lax.axis_index("xh") == 0)
    def _():
        store(0, held[0])
        store(1, held[1])

    @pl.when(lax.axis_index("xh") == 1)
    def _():
        third = pad(held[0, :part] - came[:part])
        store(0, third)
        fourth = held[1] - dot3(stack(third), (high[0], low[0]), NT)
        store(1, fourth)
        term = came[part:] - dot3(stack(fourth), (high[1], low[1]), NT)[:part]
        store(2, dot3(stack(pad(term)), (high[2], low[2]), NT))

    rows = wide[...].T.reshape(-1, 8, 128)
    lane = lax.broadcasted_iota(jnp.int32, (rows.shape[0], 1, 128), 2)
    for j in range(3):
        far = min(6 + j, 7)
        low_rows = jnp.where(lane < 80, rows[:, 3 + j : 4 + j], rows[:, far : far + 1])
        out[:, j : j + 1, :] = jnp.where(lane < 40, rows[:, j : j + 1], low_rows)


def unpack_kernel(part, got, sep, term, tall):
    for src in range(got.shape[0]):
        tall[8 * src : 8 * src + 3, :] = got[src]
        tall[8 * src + 3 : 8 * src + 6, :] = got[src]
        tall[8 * src + 6 : 8 * src + 8, :] = got[src, 0:2]
    flat = tall[...]
    row = lax.broadcasted_iota(jnp.int32, flat.shape, 0) % 8
    flat = jnp.where(
        row < 3, flat, jnp.where(row < 6, pltpu.roll(flat, 128 - 40, 1), pltpu.roll(flat, 128 - 80, 1))
    )
    lane = lax.broadcasted_iota(jnp.int32, (8, 128), 1)
    tiles = sep.shape[3] // 128
    full = [[jnp.zeros((8, 128), jnp.float32) for _ in range(tiles)] for _ in range(5)]
    for src in range(got.shape[0]):
        xl, xh, y, c = src // 32, src // 16 % 2, src // 2 % 8, src % 2
        block = flat[8 * src : 8 * src + 8]
        start = part * ((c * 2 + xl) * NY + y)
        for at in range(2 + xh):
            moved = pltpu.roll(block, (start - part * at) % 128, 1)
            to = 2 * xh + at
            for tile in range(start // 128, (start + part - 1) // 128 + 1):
                at_lane = lane + 128 * tile
                here = (at_lane >= start) & (at_lane < start + part)
                full[to][tile] = jnp.where(here, moved, full[to][tile])
    for tile in range(tiles):
        lanes = slice(128 * tile, 128 * (tile + 1))
        for k in range(4):
            sep[0, k, :, lanes] = full[k][tile]
        for layer in range(term.shape[0]):
            term[layer, :, lanes] = full[4][tile]


def in_hbm(array):
    return pltpu.with_memory_space_constraint(array, pltpu.HBM)


def in_vmem(array):
    return pltpu.with_memory_space_constraint(array, pltpu.VMEM)


def body(
    leaf_rhs,
    leaf_inverse,
    leaf_coupling,
    parent,
    sep_rhs,
    sep_inverse,
    sep_coupling,
    root_coupling,
    root_rhs,
    root_inverse,
):
    width, cols = leaf_coupling.shape[3], leaf_rhs.shape[3]
    part = cols // 32
    tiles = width // 128
    call = pl.pallas_call

    pack = call(
        pack_kernel,
        in_specs=[VMEM] * 5,
        out_specs=VMEM,
        out_shape=pltpu.VMEM((NX, 5, 8, width), jnp.float32),
        name="pack",
    )(sep_inverse, sep_coupling, root_coupling, root_rhs, root_inverse)
    exchanged = lax.all_to_all(pack, X, 0, 0)

    leaf_rhs, leaf_inverse, leaf_coupling, sep_rhs = map(
        in_hbm, (leaf_rhs, leaf_inverse, leaf_coupling, sep_rhs)
    )
    send, xt, own = leaves_send(parent, leaf_rhs, leaf_inverse, leaf_coupling, sep_rhs)
    exchanged, xt = lax.optimization_barrier((exchanged, xt))
    weights = lax.all_gather(exchanged, ("c", "y"))
    keep = leaves_keep(parent, xt, own, leaf_coupling)
    res = keep + lax.ppermute(send, "c", [(0, 1), (1, 0)])
    res = lax.all_to_all(res.reshape(NX, 2 * tiles * 8 * part, 128), X, 0, 0)
    res = call(
        sum_kernel,
        in_specs=[VMEM],
        out_specs=VMEM,
        out_shape=FLAT((8, 2 * tiles * part, 128), jnp.float32),
        compiler_params=pltpu.CompilerParams(vmem_limit_bytes=16 * 2**20),
        name="sum_x",
    )(res)
    res = lax.all_to_all(res, "y", 0, 0)

    held, send, high, low = call(
        functools.partial(first_kernel, part, cols),
        in_specs=[VMEM, HBM],
        out_specs=[VMEM] * 4,
        out_shape=[FLAT((2, 16, width), jnp.float32), FLAT((2 * part, width), jnp.float32)]
        + [FLAT((3, width, width), jnp.bfloat16)] * 2,
        scratch_shapes=[
            pltpu.VMEM((5, NX, NY, NC, 8, width), jnp.float32),
            pltpu.SemaphoreType.DMA((5, NX, NC)),
        ],
        compiler_params=pltpu.CompilerParams(vmem_limit_bytes=32 * 2**20),
        name="chain_first",
    )(res, in_hbm(weights))
    came = lax.ppermute(send, "xh", [(0, 1)])
    out = call(
        functools.partial(second_kernel, part),
        in_specs=[VMEM] * 4,
        out_specs=VMEM,
        out_shape=pltpu.VMEM((64, 3, 128), jnp.float32),
        scratch_shapes=[pltpu.VMEM((128, width), jnp.float32)],
        compiler_params=pltpu.CompilerParams(vmem_limit_bytes=16 * 2**20),
        name="chain_second",
    )(held, came, high, low)

    out = lax.all_to_all(out, ROW, 0, 0)
    sep_out, term = call(
        functools.partial(unpack_kernel, part),
        in_specs=[VMEM],
        out_specs=[VMEM] * 2,
        out_shape=[FLAT((1, 4, 8, cols), jnp.float32), pltpu.VMEM((8, 8, cols), jnp.float32)],
        scratch_shapes=[pltpu.VMEM((64 * 8, 128), jnp.float32)],
        name="unpack",
    )(in_vmem(out))
    root_out = lax.all_to_all(term, "layer", 0, 0).sum(0)
    return (sep_out, root_out)


def solution(mesh):
    fine = Mesh(mesh.devices.reshape(-1, 2, 2, NY, NC), ("layer",) + ROW)
    return jax.shard_map(
        body,
        mesh=fine,
        in_specs=(
            P("layer", ROW, None, None),
            P("layer", ROW, None, None),
            P("layer", ROW, None, None, None),
            P("layer", ROW),
            P("layer", None, ROW, None),
            P("layer", None, ROW, None),
            P("layer", None, ROW, None),
            P("layer", ROW, None),
            P(ROW, None),
            P(ROW, None),
        ),
        out_specs=(P("layer", None, ROW, None), P(ROW, None)),
        check_vma=False,
    )
```

```python
import functools

import jax
import jax.numpy as jnp
from jax import lax
from jax.experimental import pallas as pl
from jax.experimental.pallas import tpu as pltpu
from jax.sharding import Mesh, PartitionSpec as P

ROW = ("xl", "xh", "y", "c")
X = ("xl", "xh")
NX, NY, NC = 4, 8, 2
NT = (((1,), (1,)), ((), ()))
NN = (((1,), (0,)), ((), ()))
VMEM = pl.BlockSpec(memory_space=pltpu.VMEM)
SMEM = pl.BlockSpec(memory_space=pltpu.SMEM)
HBM = pl.BlockSpec(memory_space=pltpu.HBM)
FLAT = jax.ShapeDtypeStruct


def split(a):
    high = a.astype(jnp.bfloat16)
    return high, (a - high.astype(jnp.float32)).astype(jnp.bfloat16)


def stack(a):
    return jnp.concatenate(split(a), axis=0)


def dot3(a, b, dims):
    mm = functools.partial(lax.dot_general, dimension_numbers=dims, preferred_element_type=jnp.float32)
    rows = a.shape[0] // 2
    both = mm(a, b[0])
    return both[:rows] + (both[rows:] + mm(a[:rows], b[1]))


def pad(a):
    return jnp.concatenate([a, jnp.zeros((16 - a.shape[0], a.shape[1]), jnp.float32)], axis=0)


def by_tiles(ref, part):
    tiles, rows, _ = ref.shape

    def column(tile):
        return jnp.concatenate(
            [
                ref[tile, pl.ds(block + t, 8, stride=part), :]
                for block in range(0, rows, 8 * part)
                for t in range(part)
            ],
            axis=0,
        )

    return jnp.concatenate([column(tile) for tile in range(tiles)], axis=1)


def place():
    x = 2 * lax.axis_index("xl") + lax.axis_index("xh")
    return x, (x * NY + lax.axis_index("y")) * NC + lax.axis_index("c")


def pack_kernel(sep_inverse, sep_coupling, root_coupling, root_rhs, root_inverse, out):
    zeros = jnp.zeros_like(root_inverse)
    rr = jnp.concatenate([root_rhs[...], zeros[:, root_rhs.shape[1] :]], axis=1)
    tables = (
        [sep_inverse[0, 0], sep_inverse[0, 1], sep_coupling[0, 0], sep_coupling[0, 1], rr],
        [sep_inverse[0, 2], sep_inverse[0, 3], sep_coupling[0, 2], root_coupling[0], root_inverse[...]],
    )
    for x in range(out.shape[0]):
        for m in range(out.shape[1]):
            out[x, m] = tables[x % 2][m]


def half_update(part, other, parent, xt, own, coupling, out, pair):
    k = pl.program_id(0)
    core = lax.axis_index("c")
    count = xt.shape[0] // NC
    half = pl.ds(pl.multiple_of((1 - core if other else core) * count, 64), count)

    @pl.when(k == 0)
    def _():
        pair[...] = stack(xt[half, :])

    keep = jnp.where(k >= parent[0, 0], 1.0, 0.0)
    got = dot3(pair[...], split(coupling[0, 0, 0]), NT) * -keep
    block = place()[1]
    first = 8 * (block % 16)
    mine = pltpu.roll(own[half, :], (first - 8 * k + 128) % 128, 1)
    lane = lax.broadcasted_iota(jnp.int32, mine.shape, 1)
    mine = jnp.where((lane >= first) & (lane < first + 8), mine, 0.0)
    group = 8 * part
    for side in range(2):
        rows = slice(side * group, (side + 1) * group)
        for tile in range(out.shape[3]):
            out[side, 0, 0, tile] = got[rows, 128 * tile : 128 * (tile + 1)]
        out[side, 0, 0, block // 16] += mine[rows]


def send_kernel(part, parent, rhs, inv, sep, coupling, out, xt, own, plain, tall, flat, *scratch):
    @pl.when(pl.program_id(0) == 0)
    def _():
        solved = dot3(stack(inv[0, 0]), split(rhs[0, 0]), NN).T
        for tile in range(plain.shape[0]):
            plain[tile] = solved[:, 128 * tile : 128 * (tile + 1)]
        xt[...] = by_tiles(plain, part)
        tall[...] = jnp.zeros_like(tall)
        for k in range(sep.shape[1]):
            tall[8 * k : 8 * k + 8, :] = sep[0, k]
        flat[0] = tall[...].T
        own[...] = by_tiles(flat, part)

    half_update(part, True, parent, xt, own, coupling, out, *scratch)


def keep_kernel(part, parent, xt, own, coupling, out, *scratch):
    half_update(part, False, parent, xt, own, coupling, out, *scratch)


def leaf_specs(coupling, cols):
    n, width, leaf = coupling.shape[2:]
    part, tiles = cols // 32, width // 128
    one = lambda *shape: pl.BlockSpec(shape, lambda k: (0,) * len(shape))
    coupling_spec = pl.BlockSpec((1, 1, 1, width, leaf), lambda k: (0, 0, k, 0, 0))
    half_spec = pl.BlockSpec((2, 1, 1, tiles, 8 * part, 128), lambda k: (0, k // 2, k % 2, 0, 0, 0))
    half_shape = FLAT((2, 2, 2, tiles, 8 * part, 128), jnp.float32)
    shared = [one(cols, leaf), one(cols, 128)]
    pair = pltpu.VMEM((2 * (cols // NC), leaf), jnp.bfloat16)
    params = pltpu.CompilerParams(vmem_limit_bytes=24 * 2**20)
    return part, one, coupling_spec, half_spec, half_shape, shared, pair, params


def leaves_send(parent, rhs, inv, coupling, sep):
    n, leaf, cols = coupling.shape[2], rhs.shape[2], rhs.shape[3]
    part, one, coupling_spec, half_spec, half_shape, shared, pair, params = leaf_specs(coupling, cols)
    return pl.pallas_call(
        functools.partial(send_kernel, part),
        grid=(n,),
        in_specs=[SMEM, one(1, 1, leaf, cols), one(1, 1, leaf, leaf), one(1, n, 8, cols), coupling_spec],
        out_specs=[half_spec] + shared,
        out_shape=[half_shape, FLAT((cols, leaf), jnp.float32), FLAT((cols, 128), jnp.float32)],
        scratch_shapes=[
            pltpu.VMEM((leaf // 128, cols, 128), jnp.float32),
            pltpu.VMEM((128, cols), jnp.float32),
            pltpu.VMEM((1, cols, 128), jnp.float32),
            pair,
        ],
        compiler_params=params,
        name="leaves_send",
    )(parent, rhs, inv, sep, coupling)


def leaves_keep(parent, xt, own, coupling):
    part, _, coupling_spec, half_spec, half_shape, shared, pair, params = leaf_specs(coupling, xt.shape[0])
    return pl.pallas_call(
        functools.partial(keep_kernel, part),
        grid=(coupling.shape[2],),
        in_specs=[SMEM] + shared + [coupling_spec],
        out_specs=half_spec,
        out_shape=half_shape,
        scratch_shapes=[pair],
        compiler_params=params,
        name="leaves_keep",
    )(parent, xt, own, coupling)


def sum_kernel(parts, out):
    count = out.shape[1]
    for s in range(8):
        rows = pl.ds(s, count, stride=8)
        out[s] = (parts[0, rows, :] + parts[1, rows, :]) + (parts[2, rows, :] + parts[3, rows, :])


def first_kernel(part, cols, parts, weights, held, send, high, low, full, sems):
    odd = lax.axis_index("xh") == 1

    def copies(m):
        return [
            pltpu.make_async_copy(
                weights.at[:, src, m], full.at[m, pl.ds(16 * src, 16)], sems.at[m, src]
            )
            for src in range(NX)
        ]

    def matrix(m):
        for copy in copies(m):
            copy.wait()
        if m < full.shape[0] - 3:
            for copy in copies(m + 3):
                copy.start()
        return split(full[m].reshape(-1, full.shape[3]))

    for m in range(3):
        for copy in copies(m):
            copy.start()

    res = parts[0]
    for p in range(1, parts.shape[0]):
        res = res + parts[p]
    tiles = res.shape[0] // (2 * part)

    def residual(k):
        starts = [part * (tiles * k + tile) for tile in range(tiles)]
        rows = jnp.concatenate([res[at : at + part] for at in starts], axis=1)
        return stack(pad(rows))

    first = dot3(residual(0), matrix(0), NT)
    second = dot3(residual(1), matrix(1), NT)
    held[0] = first
    held[1] = second

    @pl.when(jnp.logical_not(odd))
    def _():
        chained = second - dot3(stack(first), matrix(2), NT)
        held[1] = chained
        send[:part] = dot3(stack(chained), matrix(3), NT)[:part]
        shape = (16, cols)
        group = (lax.axis_index("c") * 2 + lax.axis_index("xl")) * NY + lax.axis_index("y")
        column = lax.broadcasted_iota(jnp.int32, shape, 0) + part * group
        mine = lax.broadcasted_iota(jnp.int32, shape, 1) == column
        pick = jnp.where(mine, jnp.where(lax.axis_index("layer") == 0, 1.0, 0.0), 0.0).astype(jnp.bfloat16)
        mm = functools.partial(lax.dot_general, dimension_numbers=NT, preferred_element_type=jnp.float32)
        rhs_high, rhs_low = (half[:, :cols] for half in matrix(4))
        send[part:] = (mm(pick, rhs_high) + mm(pick, rhs_low))[:part]

    @pl.when(odd)
    def _():
        for m in range(2, full.shape[0]):
            high[m - 2], low[m - 2] = matrix(m)


def second_kernel(part, held, came, high, low, out, wide):
    wide[...] = jnp.zeros_like(wide)
    step = 40

    def store(at, value):
        for copy in range(3):
            wide[step * copy + part * at : step * copy + part * (at + 1), :] = value[:part]

    @pl.when(lax.axis_index("xh") == 0)
    def _():
        store(0, held[0])
        store(1, held[1])

    @pl.when(lax.axis_index("xh") == 1)
    def _():
        third = pad(held[0, :part] - came[:part])
        store(0, third)
        fourth = held[1] - dot3(stack(third), (high[0], low[0]), NT)
        store(1, fourth)
        term = came[part:] - dot3(stack(fourth), (high[1], low[1]), NT)[:part]
        store(2, dot3(stack(pad(term)), (high[2], low[2]), NT))

    rows = wide[...].T.reshape(-1, 8, 128)
    lane = lax.broadcasted_iota(jnp.int32, (rows.shape[0], 1, 128), 2)
    for j in range(3):
        far = min(6 + j, 7)
        low_rows = jnp.where(lane < 80, rows[:, 3 + j : 4 + j], rows[:, far : far + 1])
        out[:, j : j + 1, :] = jnp.where(lane < 40, rows[:, j : j + 1], low_rows)


def unpack_kernel(part, got, sep, term, tall):
    for src in range(got.shape[0]):
        tall[8 * src : 8 * src + 3, :] = got[src]
        tall[8 * src + 3 : 8 * src + 6, :] = got[src]
        tall[8 * src + 6 : 8 * src + 8, :] = got[src, 0:2]
    flat = tall[...]
    row = lax.broadcasted_iota(jnp.int32, flat.shape, 0) % 8
    flat = jnp.where(
        row < 3, flat, jnp.where(row < 6, pltpu.roll(flat, 128 - 40, 1), pltpu.roll(flat, 128 - 80, 1))
    )
    lane = lax.broadcasted_iota(jnp.int32, (8, 128), 1)
    tiles = sep.shape[3] // 128
    full = [[jnp.zeros((8, 128), jnp.float32) for _ in range(tiles)] for _ in range(5)]
    for src in range(got.shape[0]):
        xl, xh, y, c = src // 32, src // 16 % 2, src // 2 % 8, src % 2
        block = flat[8 * src : 8 * src + 8]
        start = part * ((c * 2 + xl) * NY + y)
        for at in range(2 + xh):
            moved = pltpu.roll(block, (start - part * at) % 128, 1)
            to = 2 * xh + at
            for tile in range(start // 128, (start + part - 1) // 128 + 1):
                at_lane = lane + 128 * tile
                here = (at_lane >= start) & (at_lane < start + part)
                full[to][tile] = jnp.where(here, moved, full[to][tile])
    for tile in range(tiles):
        lanes = slice(128 * tile, 128 * (tile + 1))
        for k in range(4):
            sep[0, k, :, lanes] = full[k][tile]
        for layer in range(term.shape[0]):
            term[layer, :, lanes] = full[4][tile]


def in_hbm(array):
    return pltpu.with_memory_space_constraint(array, pltpu.HBM)


def in_vmem(array):
    return pltpu.with_memory_space_constraint(array, pltpu.VMEM)


def body(
    leaf_rhs,
    leaf_inverse,
    leaf_coupling,
    parent,
    sep_rhs,
    sep_inverse,
    sep_coupling,
    root_coupling,
    root_rhs,
    root_inverse,
):
    width, cols = leaf_coupling.shape[3], leaf_rhs.shape[3]
    part = cols // 32
    tiles = width // 128
    call = pl.pallas_call

    pack = call(
        pack_kernel,
        in_specs=[VMEM] * 5,
        out_specs=VMEM,
        out_shape=pltpu.VMEM((NX, 5, 8, width), jnp.float32),
        name="pack",
    )(sep_inverse, sep_coupling, root_coupling, root_rhs, root_inverse)
    exchanged = lax.all_to_all(pack, X, 0, 0)

    leaf_rhs, leaf_inverse, leaf_coupling, sep_rhs = map(
        in_hbm, (leaf_rhs, leaf_inverse, leaf_coupling, sep_rhs)
    )
    send, xt, own = leaves_send(parent, leaf_rhs, leaf_inverse, leaf_coupling, sep_rhs)
    exchanged, xt = lax.optimization_barrier((exchanged, xt))
    weights = lax.all_gather(exchanged, ("y", "c"))
    keep = leaves_keep(parent, xt, own, leaf_coupling)
    res = keep + lax.ppermute(send, "c", [(0, 1), (1, 0)])
    res = lax.all_to_all(res.reshape(NX, 2 * tiles * 8 * part, 128), X, 0, 0)
    res = call(
        sum_kernel,
        in_specs=[VMEM],
        out_specs=VMEM,
        out_shape=FLAT((8, 2 * tiles * part, 128), jnp.float32),
        compiler_params=pltpu.CompilerParams(vmem_limit_bytes=16 * 2**20),
        name="sum_x",
    )(res)
    res = lax.all_to_all(res, "y", 0, 0)

    held, send, high, low = call(
        functools.partial(first_kernel, part, cols),
        in_specs=[VMEM, HBM],
        out_specs=[VMEM] * 4,
        out_shape=[FLAT((2, 16, width), jnp.float32), FLAT((2 * part, width), jnp.float32)]
        + [FLAT((3, width, width), jnp.bfloat16)] * 2,
        scratch_shapes=[pltpu.VMEM((5, 64, 8, width), jnp.float32), pltpu.SemaphoreType.DMA((5, NX))],
        compiler_params=pltpu.CompilerParams(vmem_limit_bytes=32 * 2**20),
        name="chain_first",
    )(res, in_hbm(weights))
    came = lax.ppermute(send, "xh", [(0, 1)])
    out = call(
        functools.partial(second_kernel, part),
        in_specs=[VMEM] * 4,
        out_specs=VMEM,
        out_shape=pltpu.VMEM((64, 3, 128), jnp.float32),
        scratch_shapes=[pltpu.VMEM((128, width), jnp.float32)],
        compiler_params=pltpu.CompilerParams(vmem_limit_bytes=16 * 2**20),
        name="chain_second",
    )(held, came, high, low)

    out = lax.all_to_all(out, ROW, 0, 0)
    sep_out, term = call(
        functools.partial(unpack_kernel, part),
        in_specs=[VMEM],
        out_specs=[VMEM] * 2,
        out_shape=[FLAT((1, 4, 8, cols), jnp.float32), pltpu.VMEM((8, 8, cols), jnp.float32)],
        scratch_shapes=[pltpu.VMEM((64 * 8, 128), jnp.float32)],
        name="unpack",
    )(in_vmem(out))
    root_out = lax.all_to_all(term, "layer", 0, 0).sum(0)
    return (sep_out, root_out)


def solution(mesh):
    fine = Mesh(mesh.devices.reshape(-1, 2, 2, NY, NC), ("layer",) + ROW)
    return jax.shard_map(
        body,
        mesh=fine,
        in_specs=(
            P("layer", ROW, None, None),
            P("layer", ROW, None, None),
            P("layer", ROW, None, None, None),
            P("layer", ROW),
            P("layer", None, ROW, None),
            P("layer", None, ROW, None),
            P("layer", None, ROW, None),
            P("layer", ROW, None),
            P(ROW, None),
            P(ROW, None),
        ),
        out_specs=(P("layer", None, ROW, None), P(ROW, None)),
        check_vma=False,
    )
```
